128 devices in a mesh: seq: 32 (over z, x, core), tp: 4 (over y).
Axes of the slice: x: 4, y: 4, z: 4, core: 2. Of those that a mesh axis runs over, the one named last changes fastest.
Arguments:
- frames: bfloat16 [8192, 1280], P('seq'), may hold values from -6 to 6
- gain_attn: float32 [1280], replicated, may hold values from 0.1 to 1.9
- w_qkv: bfloat16 [3, 1280, 1280], P(None, None, 'tp'), as said below
- w_out: bfloat16 [1280, 1280], P('tp'), may hold values from -0.15625 to 0.15625
- gain_ffn: float32 [1280], replicated, may hold values from 0.1 to 1.9
- w_up: bfloat16 [1280, 5120], P(None, 'tp'), may hold values from -0.15625 to 0.15625
- w_down: bfloat16 [5120, 1280], P('tp'), may hold values from -0.078125 to 0.078125
- w_conv: bfloat16 [3, 1280, 1280], P(None, None, 'tp'), may hold values from -0.09375 to 0.09375
- w_proj: bfloat16 [1280, 4096], P('tp'), may hold values from -0.15625 to 0.15625
- block_utt: int32 [64], P('seq'), may hold values from 0 to 15, never falling along the last dimension, each value on 1 to 11 neighbouring positions
Outputs:
- lm_rows: bfloat16 [4096, 4096], P(('seq', 'tp'))
The draws below stay inside these ranges and needn't reach their ends.
Inputs may be any that keep to these rules, and one draw needn't show every extreme that they name: `block_utt`: ids never fall from block to block; each utterance covers 1 to 11 consecutive blocks, every id is used, and one utterance covers exactly 11 blocks. `w_qkv`: entries of order a few times 1280 ** -0.5.
All inputs are finite; a program needn't handle non-finite values.
Results may differ from the reference program's by a relative error of at most 0.025.
The reference program's roundings to bfloat16 on the way (of `normed`, `attended`, `normed_two`, `hidden`, `layer_out` and `pooled`) count: a program that leaves them out, or rounds other values in their place, can miss the bound.
Values may be sent and summed in bfloat16 or wider, within the bound.
No kernel may reach another device: no remote copies, remote signals or barrier semaphores. Data moves between devices by JAX's collectives and lax.ppermute only.
A program may use at most 64 MiB of HBM per device.

```python
import math
import jax
import jax.numpy as jnp
import numpy as np
from jax import lax

D = 1280
HEADS = 20
HEAD_DIM = 64
FF = 5120
LM_D = 4096
FRAME_BLK = 128
MOST_BLK = 11
FR_DEV = 256
FRAMES = 8192
NBLK = 64
UTTS = 16
POOLED = 4096


def draw_frames(key, part):
    key = jax.random.fold_in(key, 11)
    period = 9 * FRAME_BLK
    half = D // 2
    table = jax.random.normal(jax.random.fold_in(key, 1), (2 * period, half), jnp.float32)
    positions = jnp.arange(FRAMES, dtype=jnp.int32)
    front_index = positions % (2 * period)
    back_index = (positions + period) % (2 * period)
    planted = jnp.concatenate([table[front_index], table[back_index]], axis=1)
    noise_key = jax.random.fold_in(key, 2)
    noise = jax.random.normal(noise_key, (FRAMES, D), jnp.float32)
    mixed = math.sqrt(0.2) * noise + math.sqrt(0.8) * planted
    return jnp.clip(mixed, -6.0, 6.0).astype(jnp.bfloat16)


def draw_w_qkv(key, part):
    key = jax.random.fold_in(key, 7)
    half = D // 2
    shared = jax.random.normal(jax.random.fold_in(key, 1), (half, D), jnp.float32) * (3.0 * D ** (-0.5))
    query_rest = jax.random.normal(jax.random.fold_in(key, 2), (half, D), jnp.float32) * D ** (-0.5)
    key_rest = jax.random.normal(jax.random.fold_in(key, 3), (half, D), jnp.float32) * D ** (-0.5)
    value_part = jax.random.normal(jax.random.fold_in(key, 4), (D, D), jnp.float32) * D ** (-0.5)
    query_part = jnp.concatenate([shared, query_rest], axis=0)
    key_part = jnp.concatenate([key_rest, shared], axis=0)
    return jnp.stack([query_part, key_part, value_part], axis=0).astype(jnp.bfloat16)


def shard_levels(rng, shape, cuts, smallest, top_value):
    factor_of, own = 1.0, jax.random.fold_in(rng, 6)
    for dim, blocks in cuts:
        heights = jnp.exp(jax.random.uniform(jax.random.fold_in(own, dim), (blocks,), jnp.float32, smallest / len(cuts), top_value / len(cuts)))
        factor_of = factor_of * jnp.repeat(heights, shape[dim] // blocks).reshape([-1 if axis == dim else 1 for axis in range(len(shape))])
    return factor_of


def profile(count, total, bound, lean):
    loads = [(1 << 20) // math.isqrt(rank ** lean) + 1 for rank in range(2, count + 1)]
    spare, holding = total - bound - (count - 1), [1] * (count - 1)
    while spare > 0:
        candidates = [i for i in range(count - 1) if holding[i] < bound]
        whole, remaining = sum([loads[i] for i in candidates]), spare
        for i in candidates:
            more = min(bound - holding[i], max(1, remaining * loads[i] // whole), spare)
            holding[i] = holding[i] + more
            spare = spare - more
    return np.array([bound] + holding)


def uneven_parts(stream_key, number_of, total, reach, lean):
    if number_of == 2:
        one = jax.random.randint(stream_key, (), max(1, total - reach), min(reach, total - 1) + 1)
        return jnp.stack([one, total - one])
    sizes = jnp.asarray(profile(number_of, total, reach, lean), jnp.int32)
    couples = (number_of - 1) // 2
    source_of, sink = sizes[1:1 + 2 * couples:2], sizes[2:2 + 2 * couples:2]
    slack = jnp.minimum(source_of - 1, reach - sink)
    moved = jax.random.randint(jax.random.fold_in(stream_key, 1), (couples,), 0, 1 << 20) % (slack + 1)
    sizes = sizes.at[1:1 + 2 * couples:2].set(source_of - moved).at[2:2 + 2 * couples:2].set(sink + moved)
    return sizes[jax.random.permutation(jax.random.fold_in(stream_key, 2), number_of)]


def scatter_about(own_key, shape, deviation, limit, shards=(), kind=jnp.bfloat16):
    level = shard_levels(own_key, shape, shards, -0.22, 0.18) if shards else 1.0
    values = jax.random.normal(own_key, shape, jnp.float32) * deviation * level
    return jnp.minimum(jnp.maximum(values, -limit), limit).astype(kind)


def setup_inputs(seed: int = 0) -> dict:
    streams_of = jax.random.split(jax.random.key(seed), 11)
    return {
        "frames": draw_frames(jax.random.fold_in(streams_of[10], 71), 0),
        "gain_attn": jnp.clip(1.0 + 0.18 * jax.random.normal(streams_of[1], (D,), jnp.float32), 0.1, 1.9),
        "w_qkv": draw_w_qkv(jax.random.fold_in(streams_of[10], 71), 0),
        "w_out": scatter_about(streams_of[3], (D, D), D ** -0.5, 0.15625, ((0, 4),)),
        "gain_ffn": jnp.clip(1.0 + 0.18 * jax.random.normal(streams_of[4], (D,), jnp.float32), 0.1, 1.9),
        "w_up": scatter_about(streams_of[5], (D, FF), D ** -0.5, 0.15625, ((1, 4),)),
        "w_down": scatter_about(streams_of[6], (FF, D), FF ** -0.5, 0.078125, ((0, 4),)),
        "w_conv": scatter_about(streams_of[7], (3, D, D), (3 * D) ** -0.5, 0.09375, ((2, 4),)),
        "w_proj": scatter_about(streams_of[8], (D, LM_D), D ** -0.5, 0.15625, ((0, 4),)),
        "block_utt": jnp.searchsorted(jnp.cumsum(uneven_parts(streams_of[9], UTTS, NBLK, MOST_BLK, 2)), jnp.arange(NBLK), side="right").astype(jnp.int32),
    }


def layer_norm(value, gain):
    mean = lax.optimization_barrier(jnp.mean(value, axis=-1, keepdims=True))
    centred = value - mean
    spread = lax.optimization_barrier(jnp.mean(centred * centred, axis=-1, keepdims=True))
    return centred * lax.rsqrt(spread + 1e-05) * gain

def reference(frames, gain_attn, w_qkv, w_out, gain_ffn, w_up, w_down, w_conv, w_proj, block_utt):
    frame_id = (jnp.repeat(block_utt, FRAME_BLK) + 1).astype(jnp.int32)
    resid_in = frames.astype(jnp.float32)
    normed = layer_norm(resid_in, gain_attn).astype(jnp.bfloat16)
    queries = jnp.dot(normed, w_qkv[0], preferred_element_type=jnp.float32).astype(jnp.bfloat16)
    keys = jnp.dot(normed, w_qkv[1], preferred_element_type=jnp.float32).astype(jnp.bfloat16)
    values = jnp.dot(normed, w_qkv[2], preferred_element_type=jnp.float32).astype(jnp.bfloat16)
    keys_all = keys.astype(jnp.float32).reshape(FRAMES, HEADS, HEAD_DIM)
    values_all = values.astype(jnp.float32).reshape(FRAMES, HEADS, HEAD_DIM)
    blocks = FRAMES // FR_DEV
    query_blocks = queries.astype(jnp.float32).reshape(blocks, FR_DEV, HEADS, HEAD_DIM)
    id_blocks = frame_id.reshape(blocks, FR_DEV)

    def attend(item):
        query_part, id_part = item
        scores = jnp.einsum('fhd,ghd->fhg', query_part, keys_all) / HEAD_DIM ** 0.5
        same = (id_part[:, None] == frame_id[None, :])[:, None, :]
        scores = jnp.where(same, scores, -1e+30)
        top = lax.optimization_barrier(jnp.max(scores, axis=-1, keepdims=True))
        weights = jnp.where(same, jnp.exp(scores - top), 0.0)
        total = lax.optimization_barrier(jnp.sum(weights, axis=-1))
        rounded = weights.astype(jnp.bfloat16).astype(jnp.float32)
        summed = jnp.einsum('fhg,ghd->fhd', rounded, values_all)
        return (summed / total[..., None]).reshape(FR_DEV, D)
    attended = lax.map(attend, (query_blocks, id_blocks)).reshape(FRAMES, D).astype(jnp.bfloat16)
    resid = resid_in + jnp.dot(attended, w_out, preferred_element_type=jnp.float32)
    normed_two = layer_norm(resid, gain_ffn).astype(jnp.bfloat16)
    hidden = jax.nn.gelu(jnp.dot(normed_two, w_up, preferred_element_type=jnp.float32), approximate=False).astype(jnp.bfloat16)
    layer_out = (resid + jnp.dot(hidden, w_down, preferred_element_type=jnp.float32)).astype(jnp.bfloat16)
    pairs = layer_out.reshape(POOLED, 2, D)
    pair_ids = frame_id.reshape(POOLED, 2)
    even_rows = pairs[:, 0]
    odd_rows = pairs[:, 1]
    before = jnp.concatenate([jnp.zeros((1, D), jnp.bfloat16), odd_rows[:-1]], axis=0)
    before_ids = jnp.concatenate([jnp.zeros((1,), jnp.int32), pair_ids[:-1, 1]], axis=0)
    keep_before = (before_ids == pair_ids[:, 0]).astype(jnp.bfloat16)[:, None]
    keep_after = (pair_ids[:, 1] == pair_ids[:, 0]).astype(jnp.bfloat16)[:, None]
    conv = jnp.dot(before * keep_before, w_conv[0], preferred_element_type=jnp.float32)
    conv = conv + jnp.dot(even_rows, w_conv[1], preferred_element_type=jnp.float32)
    conv = conv + jnp.dot(odd_rows * keep_after, w_conv[2], preferred_element_type=jnp.float32)
    pooled = jax.nn.gelu(conv, approximate=False).astype(jnp.bfloat16)
    return jnp.dot(pooled, w_proj, preferred_element_type=jnp.float32).astype(jnp.bfloat16)
```

```python
import jax
import jax.numpy as jnp
from jax import lax
from jax.experimental import pallas as pl
from jax.experimental.pallas import tpu as pltpu
from jax.sharding import PartitionSpec as P

HEAD_DIM = 64
BLK = 128
MOST = 11
IDROWS = 16
SEQ = "seq"
TP = "tp"
VMEM = pl.BlockSpec(memory_space=pltpu.VMEM)
SMEM = pl.BlockSpec(memory_space=pltpu.SMEM)
ANY = pl.BlockSpec(memory_space=pl.ANY)


def send_tp(value, steps):
    count = lax.axis_size(TP)
    return lax.ppermute(value, TP, [(t, (t + steps) % count) for t in range(count)])


def send_seq(value, steps):
    count = lax.axis_size(SEQ)
    return lax.ppermute(
        value, SEQ, [(s, s + steps) for s in range(count) if 0 <= s + steps < count]
    )


def send_partner(value):
    count = lax.axis_size(SEQ)
    return lax.ppermute(value, SEQ, [(s, s ^ 1) for s in range(count)])


def send_five(value):
    count = lax.axis_size(SEQ)
    pairs = [(s, s + 5 if s % 2 else s - 5) for s in range(count)]
    return lax.ppermute(value, SEQ, [(a, b) for a, b in pairs if 0 <= b < count])


def layer_norm(value, gain):
    mean = jnp.mean(value, axis=-1, keepdims=True)
    centred = value - mean
    spread = jnp.mean(centred * centred, axis=-1, keepdims=True)
    return centred * lax.rsqrt(spread + 1e-05) * gain


def kv_kernel(ids_ref, frames_ref, gain_ref, w_ref, normed_ref, kv_ref):
    rows = frames_ref.shape[0]
    normed = layer_norm(frames_ref[...].astype(jnp.float32), gain_ref[...]).astype(jnp.bfloat16)
    normed_ref[...] = normed
    keys = jnp.dot(normed, w_ref[1], preferred_element_type=jnp.float32).astype(jnp.bfloat16)
    values = jnp.dot(normed, w_ref[2], preferred_element_type=jnp.float32).astype(jnp.bfloat16)
    kv_ref[:rows, :256] = keys[:, :256]
    kv_ref[:rows, 256:512] = values[:, :256]
    kv_ref[:rows, 512:576] = keys[:, 256:]
    kv_ref[:rows, 576:] = values[:, 256:]
    row = lax.broadcasted_iota(jnp.int32, (IDROWS, kv_ref.shape[1]), 0)
    marks = jnp.where(row == 0, ids_ref[0] + 1, jnp.where(row == 1, ids_ref[1] + 1, 0))
    kv_ref[rows:, :] = marks.astype(jnp.float32).astype(jnp.bfloat16)


def attend_kernel(info_ref, q_ref, *refs):
    pieces, (out_ref, buf, marks, sems, mark_sems) = refs[:11], refs[11:]
    parity = info_ref[2]
    rows = q_ref.shape[0]
    copies = []
    for n, piece in enumerate(pieces):
        if n < 5:
            slot = 1 + 2 * n + parity
        elif n < 10:
            slot = 2 * (n - 4) - parity
        else:
            slot = 11 * parity
        copies.append(pltpu.make_async_copy(
            piece.at[pl.ds(rows, IDROWS), pl.ds(0, 128)], marks.at[slot], mark_sems.at[n]))
        copies.append(pltpu.make_async_copy(
            piece.at[pl.ds(0, rows), :], buf.at[pl.ds(pl.multiple_of(slot * rows, rows), rows), :], sems.at[n]))
    for copy in copies:
        copy.start()
    unused = 11 - 11 * parity
    marks[unused] = jnp.zeros(marks.shape[1:], marks.dtype)
    for copy in copies:
        copy.wait()
    seen = marks[...].astype(jnp.float32)
    row = lax.broadcasted_iota(jnp.int32, seen.shape, 1)
    place = (2 * lax.broadcasted_iota(jnp.int32, seen.shape, 0) + row).astype(jnp.float32)
    lane = lax.broadcasted_iota(jnp.int32, (BLK, 128), 1)
    column = lax.broadcasted_iota(jnp.int32, (1, MOST * BLK), 1)
    low = lane < HEAD_DIM
    for i in range(2):
        mine = (info_ref[i] + 1).astype(jnp.float32)
        same = (seen == mine) & (row < 2)
        first = jnp.min(jnp.where(same, place, 99.0)).astype(jnp.int32)
        last = jnp.max(jnp.where(same, place, -1.0)).astype(jnp.int32)
        start = jnp.clip(first, 2 * parity, MOST + 2 * parity)
        begin = pl.multiple_of(start * BLK, BLK)
        kept = (last + 1 - start) * BLK
        bias = jnp.where(column < kept, 0.0, -1e30)
        window = pl.ds(begin, MOST * BLK)
        for pair in range(3):
            if pair < 2:
                q_pair = q_ref[i * BLK:(i + 1) * BLK, pair * 128:(pair + 1) * 128]
                keys = buf[window, pair * 128:(pair + 1) * 128]
                values = buf[window, 256 + pair * 128:256 + (pair + 1) * 128]
            else:
                q_pair = q_ref[i * BLK:(i + 1) * BLK, 256:384]
                keys = buf[window, 512:640]
                values = keys
            q_pair = q_pair * jnp.asarray(HEAD_DIM ** -0.5, q_pair.dtype)
            halves = []
            for half in range(2 if pair < 2 else 1):
                q_head = jnp.where(low if half == 0 else ~low, q_pair, jnp.zeros_like(q_pair))
                scores = lax.dot_general(
                    q_head, keys, (((1,), (1,)), ((), ())), preferred_element_type=jnp.float32) + bias
                top = jnp.max(scores, axis=-1, keepdims=True)
                weights = jnp.exp(scores - top)
                total = jnp.sum(weights, axis=-1, keepdims=True)
                summed = jnp.dot(weights.astype(jnp.bfloat16), values, preferred_element_type=jnp.float32)
                halves.append(summed / total)
            if pair < 2:
                merged = jnp.where(low, halves[0], halves[1])
                out_ref[i * BLK:(i + 1) * BLK, pair * 128:(pair + 1) * 128] = merged.astype(jnp.bfloat16)
            else:
                out_ref[i * BLK:(i + 1) * BLK, 256:] = halves[0][:, HEAD_DIM:].astype(jnp.bfloat16)


def attend(ids, normed, w_query, kv):
    rows = normed.shape[0]
    parity = lax.rem(lax.axis_index(SEQ), 2)
    far_back, far_on = send_seq(kv, 4), send_seq(kv, -4)
    back, on = send_seq(kv, 2), send_seq(kv, -2)
    five = send_five(kv)
    beside = send_partner(kv)
    queries = jnp.dot(normed, jnp.pad(w_query, ((0, 0), (0, 64))), preferred_element_type=jnp.float32).astype(jnp.bfloat16)
    chain = [far_back, back, kv, on, far_on]
    swapped = [send_partner(far_back), send_partner(back), beside, send_partner(on), send_partner(far_on)]
    info = jnp.concatenate([ids, parity[None].astype(jnp.int32)])
    return pl.pallas_call(
        attend_kernel,
        out_shape=jax.ShapeDtypeStruct((rows, w_query.shape[1]), jnp.bfloat16),
        in_specs=[SMEM, VMEM] + [ANY] * 11,
        out_specs=VMEM,
        scratch_shapes=[
            pltpu.VMEM((12 * rows, kv.shape[1]), jnp.bfloat16),
            pltpu.VMEM((12, IDROWS, 128), jnp.bfloat16),
            pltpu.SemaphoreType.DMA((11,)),
            pltpu.SemaphoreType.DMA((11,)),
        ],
        compiler_params=pltpu.CompilerParams(vmem_limit_bytes=24 << 20),
        cost_estimate=pl.CostEstimate(flops=1 << 30, bytes_accessed=4 << 20, transcendentals=1 << 21),
    )(info, queries, *chain, *swapped, five)


def shards(frames, gain_attn, w_qkv, w_out, gain_ffn, w_up, w_down, w_conv, w_proj, block_utt):
    rows, width = frames.shape
    tp = lax.axis_index(TP)
    core = lax.rem(lax.axis_index(SEQ), 2)
    resid_in = frames.astype(jnp.float32)
    normed, kv = pl.pallas_call(
        kv_kernel,
        out_shape=(
            jax.ShapeDtypeStruct((rows, width), jnp.bfloat16),
            jax.ShapeDtypeStruct((rows + IDROWS, 2 * w_qkv.shape[2]), jnp.bfloat16),
        ),
        in_specs=[SMEM, VMEM, VMEM, VMEM],
        out_specs=(VMEM, VMEM),
        compiler_params=pltpu.CompilerParams(vmem_limit_bytes=16 << 20),
        cost_estimate=pl.CostEstimate(flops=1 << 29, bytes_accessed=4 << 20, transcendentals=0),
    )(block_utt, frames, gain_attn[None], w_qkv)
    attended = attend(block_utt, normed, w_qkv[0], kv)

    half = width // 2
    mine = lax.dynamic_slice_in_dim(w_out, core * half, half, axis=1)
    fetched = jnp.stack([send_tp(mine, k) for k in (1, 2, 3)])
    other = send_partner(fetched)
    left = jnp.where(core == 0, fetched, other)
    right = jnp.where(core == 0, other, fetched)

    heads = [attended] + [send_tp(attended, k) for k in (1, 2, 3)]
    term = jnp.dot(heads[0], w_out, preferred_element_type=jnp.float32)
    for k in range(3):
        both = jnp.concatenate([left[k], right[k]], axis=1)
        term = term + jnp.dot(heads[k + 1], both, preferred_element_type=jnp.float32)
    resid = resid_in + term
    normed_two = layer_norm(resid, gain_ffn).astype(jnp.bfloat16)
    hidden = jax.nn.gelu(
        jnp.dot(normed_two, w_up, preferred_element_type=jnp.float32), approximate=False
    ).astype(jnp.bfloat16)
    ffn_term = jnp.dot(hidden, w_down, preferred_element_type=jnp.float32).astype(jnp.bfloat16)

    share = rows // 4
    parts = ffn_term.reshape(4, share, width)
    pick = lambda array, k: lax.dynamic_index_in_dim(array, lax.rem(tp + k, 4), 0, False)
    got = [send_tp(pick(parts, k), k) for k in (1, 2, 3)]
    total = pick(resid.reshape(4, share, width), 0) + pick(parts, 0).astype(jnp.float32)
    for piece in got:
        total = total + piece.astype(jnp.float32)
    own = total.astype(jnp.bfloat16)
    spread = jnp.stack([own] + [send_tp(own, 4 - k) for k in (1, 2, 3)])
    layer_out = jnp.concatenate([spread, spread])
    layer_out = lax.dynamic_slice_in_dim(layer_out, lax.rem(4 - tp, 4), 4, 0).reshape(rows, width)

    frame_id = jnp.repeat(block_utt, BLK, total_repeat_length=rows) + 1
    rim_frame = send_seq(layer_out[-1:], 1)
    rim_id = send_seq(frame_id[-1:], 1)
    pooled_count = rows // 2
    pairs = layer_out.reshape(pooled_count, 2, width)
    pair_ids = frame_id.reshape(pooled_count, 2)
    even_rows = pairs[:, 0]
    odd_rows = pairs[:, 1]
    before = jnp.concatenate([rim_frame, odd_rows[:-1]], axis=0)
    before_ids = jnp.concatenate([rim_id, pair_ids[:-1, 1]], axis=0)
    keep_before = (before_ids == pair_ids[:, 0]).astype(jnp.bfloat16)[:, None]
    conv = jnp.dot(before * keep_before, w_conv[0], preferred_element_type=jnp.float32)
    conv = conv + jnp.dot(even_rows, w_conv[1], preferred_element_type=jnp.float32)
    conv = conv + jnp.dot(odd_rows, w_conv[2], preferred_element_type=jnp.float32)
    pooled = jax.nn.gelu(conv, approximate=False).astype(jnp.bfloat16)
    lm = jnp.dot(pooled, w_proj, preferred_element_type=jnp.float32).astype(jnp.bfloat16)
    lm = lm.reshape(4, pooled_count // 4, w_proj.shape[1])
    got = [send_tp(pick(lm, k), k) for k in (1, 2, 3)]
    total = pick(lm, 0).astype(jnp.float32)
    for piece in got:
        total = total + piece.astype(jnp.float32)
    return total.astype(jnp.bfloat16)


def solution(mesh):
    placed = (
        P("seq", None),
        P(),
        P(None, None, "tp"),
        P("tp", None),
        P(),
        P(None, "tp"),
        P("tp", None),
        P(None, None, "tp"),
        P("tp", None),
        P("seq"),
    )
    return jax.shard_map(
        shards, mesh=mesh, in_specs=placed, out_specs=P(("seq", "tp"), None), check_vma=False
    )
```

```python
import jax
import jax.numpy as jnp
from jax import lax
from jax.experimental import pallas as pl
from jax.experimental.pallas import tpu as pltpu
from jax.sharding import PartitionSpec as P

HEAD_DIM = 64
BLK = 128
MOST = 11
IDROWS = 16
SEQ = "seq"
TP = "tp"
VMEM = pl.BlockSpec(memory_space=pltpu.VMEM)
SMEM = pl.BlockSpec(memory_space=pltpu.SMEM)
ANY = pl.BlockSpec(memory_space=pl.ANY)


def send_tp(value, steps):
    count = lax.axis_size(TP)
    return lax.ppermute(value, TP, [(t, (t + steps) % count) for t in range(count)])


def send_seq(value, steps):
    count = lax.axis_size(SEQ)
    return lax.ppermute(
        value, SEQ, [(s, s + steps) for s in range(count) if 0 <= s + steps < count]
    )


def send_partner(value):
    count = lax.axis_size(SEQ)
    return lax.ppermute(value, SEQ, [(s, s ^ 1) for s in range(count)])


def send_five(value):
    count = lax.axis_size(SEQ)
    pairs = [(s, s + 5 if s % 2 else s - 5) for s in range(count)]
    return lax.ppermute(value, SEQ, [(a, b) for a, b in pairs if 0 <= b < count])


def layer_norm(value, gain):
    mean = jnp.mean(value, axis=-1, keepdims=True)
    centred = value - mean
    spread = jnp.mean(centred * centred, axis=-1, keepdims=True)
    return centred * lax.rsqrt(spread + 1e-05) * gain


def dot_t(left, right):
    return lax.dot_general(left, right, (((1,), (1,)), ((), ())), preferred_element_type=jnp.float32)


def dot(left, right):
    return jnp.dot(left, right, preferred_element_type=jnp.float32)


def gelu(value):
    return 0.5 * value * (1.0 + lax.erf(value * (0.5 ** 0.5)))


def kv_kernel(ids_ref, frames_ref, gain_ref, w_ref, normed_ref, kv_ref):
    rows = frames_ref.shape[0]
    normed = layer_norm(frames_ref[...].astype(jnp.float32), gain_ref[...]).astype(jnp.bfloat16)
    normed_ref[...] = normed
    keys = dot_t(normed, w_ref[1]).astype(jnp.bfloat16)
    values = dot_t(normed, w_ref[2]).astype(jnp.bfloat16)
    kv_ref[:rows, :256] = keys[:, :256]
    kv_ref[:rows, 256:512] = values[:, :256]
    kv_ref[:rows, 512:576] = keys[:, 256:]
    kv_ref[:rows, 576:] = values[:, 256:]
    row = lax.broadcasted_iota(jnp.int32, (IDROWS, kv_ref.shape[1]), 0)
    marks = jnp.where(row == 0, ids_ref[0] + 1, jnp.where(row == 1, ids_ref[1] + 1, 0))
    kv_ref[rows:, :] = marks.astype(jnp.float32).astype(jnp.bfloat16)


def attend_kernel(info_ref, q_ref, *refs):
    pieces, (out_ref, joined_ref, buf, marks, sems, mark_sems) = refs[:11], refs[11:]
    parity = info_ref[2]
    rows = q_ref.shape[0]
    copies = []
    for n, piece in enumerate(pieces):
        if n < 5:
            slot = 1 + 2 * n + parity
        elif n < 10:
            slot = 2 * (n - 4) - parity
        else:
            slot = 11 * parity
        copies.append(pltpu.make_async_copy(
            piece.at[pl.ds(rows, IDROWS), pl.ds(0, 128)], marks.at[slot], mark_sems.at[n]))
        copies.append(pltpu.make_async_copy(
            piece.at[pl.ds(0, rows), :], buf.at[pl.ds(pl.multiple_of(slot * rows, rows), rows), :], sems.at[n]))
    for copy in copies:
        copy.start()
    unused = 11 - 11 * parity
    marks[unused] = jnp.zeros(marks.shape[1:], marks.dtype)
    for copy in copies:
        copy.wait()
    seen = marks[...].astype(jnp.float32)
    row = lax.broadcasted_iota(jnp.int32, seen.shape, 1)
    place = (2 * lax.broadcasted_iota(jnp.int32, seen.shape, 0) + row).astype(jnp.float32)
    lane = lax.broadcasted_iota(jnp.int32, (BLK, 128), 1)
    column = lax.broadcasted_iota(jnp.int32, (1, MOST * BLK), 1)
    low = lane < HEAD_DIM
    for i in range(2):
        mine = (info_ref[i] + 1).astype(jnp.float32)
        same = (seen == mine) & (row < 2)
        first = jnp.min(jnp.where(same, place, 99.0)).astype(jnp.int32)
        last = jnp.max(jnp.where(same, place, -1.0)).astype(jnp.int32)
        if i == 0:
            joined_ref[0] = (first < 10 + 2 * parity).astype(jnp.int32)
        start = jnp.clip(first, 2 * parity, MOST + 2 * parity)
        begin = pl.multiple_of(start * BLK, BLK)
        kept = (last + 1 - start) * BLK
        bias = jnp.where(column < kept, 0.0, -1e30)
        window = pl.ds(begin, MOST * BLK)
        for pair in range(3):
            if pair < 2:
                q_pair = q_ref[i * BLK:(i + 1) * BLK, pair * 128:(pair + 1) * 128]
                keys = buf[window, pair * 128:(pair + 1) * 128]
                values = buf[window, 256 + pair * 128:256 + (pair + 1) * 128]
            else:
                q_pair = q_ref[i * BLK:(i + 1) * BLK, 256:384]
                keys = buf[window, 512:640]
                values = keys
            q_pair = q_pair * jnp.asarray(HEAD_DIM ** -0.5, q_pair.dtype)
            halves = []
            for half in range(2 if pair < 2 else 1):
                q_head = jnp.where(low if half == 0 else ~low, q_pair, jnp.zeros_like(q_pair))
                scores = lax.dot_general(
                    q_head, keys, (((1,), (1,)), ((), ())), preferred_element_type=jnp.float32) + bias
                top = jnp.max(scores, axis=-1, keepdims=True)
                weights = jnp.exp(scores - top)
                total = jnp.sum(weights, axis=-1, keepdims=True)
                summed = jnp.dot(weights.astype(jnp.bfloat16), values, preferred_element_type=jnp.float32)
                halves.append(summed / total)
            if pair < 2:
                merged = jnp.where(low, halves[0], halves[1])
                out_ref[i * BLK:(i + 1) * BLK, pair * 128:(pair + 1) * 128] = merged.astype(jnp.bfloat16)
            else:
                out_ref[i * BLK:(i + 1) * BLK, 256:] = halves[0][:, HEAD_DIM:].astype(jnp.bfloat16)


def query_kernel(normed_ref, w_ref, q_ref):
    q_ref[...] = jnp.zeros_like(q_ref)
    q_ref[:, :w_ref.shape[1]] = dot_t(normed_ref[...], w_ref[0]).astype(jnp.bfloat16)


def mlp_kernel(tp_ref, att0, att1, att2, att3, w_out_ref, frames_ref, gain_ref, w_up_ref, w_down_ref,
               resid_ref, part0, part1, part2, part3, resid_all, part_all):
    tp = tp_ref[0]
    rows, heads = att0.shape
    share = rows // 4
    resid = frames_ref[...].astype(jnp.float32)
    for k, att in enumerate((att0, att1, att2, att3)):
        source = lax.rem(tp + 4 - k, 4)
        resid = resid + dot(att[...], w_out_ref[pl.ds(pl.multiple_of(source * heads, heads), heads), :])
    resid_all[...] = resid
    normed = layer_norm(resid, gain_ref[...]).astype(jnp.bfloat16)
    hidden = gelu(dot(normed, w_up_ref[...])).astype(jnp.bfloat16)
    part_all[...] = dot(hidden, w_down_ref[...]).astype(jnp.bfloat16)
    mine = pl.ds(pl.multiple_of(tp * share, share), share)
    resid_ref[:share, :] = resid_all[mine, :]
    resid_ref[share:, :] = resid_all[rows - IDROWS:, :]
    for k, part in enumerate((part0, part1, part2, part3)):
        target = lax.rem(tp + k, 4)
        part[:share, :] = part_all[pl.ds(pl.multiple_of(target * share, share), share), :]
        part[share:, :] = part_all[rows - IDROWS:, :]


def layer_sum_kernel(resid_ref, own, got1, got2, got3, out_ref, rim_ref):
    total = resid_ref[...] + own[...].astype(jnp.float32)
    for piece in (got1, got2, got3):
        total = total + piece[...].astype(jnp.float32)
    share = out_ref.shape[0]
    out_ref[...] = total[:share].astype(jnp.bfloat16)
    rim_ref[...] = total[share:].astype(jnp.bfloat16)


def adapter_kernel(info_ref, own, got1, got2, got3, rim_ref, w_conv_ref, w_proj_ref,
                   lm0, lm1, lm2, lm3, rows_ref, pooled_ref):
    tp = info_ref[0]
    share = own.shape[0]
    for k, piece in enumerate((own, got1, got2, got3)):
        source = lax.rem(tp + 4 - k, 4)
        rows_ref[pl.ds(pl.multiple_of(source * share, share), share), :] = piece[...]
    rows = rows_ref[...]
    count = rows.shape[0] // 2
    j = lax.broadcasted_iota(jnp.int32, (count, 2 * count), 0)
    r = lax.broadcasted_iota(jnp.int32, (count, 2 * count), 1)
    same_block = info_ref[1] == info_ref[2]
    cut = jnp.where(same_block, -1, count // 2)
    one = lambda flag: jnp.where(flag, 1.0, 0.0).astype(jnp.bfloat16)
    pick = lambda flag, source: dot(one(flag), source).astype(jnp.bfloat16)
    even = pick(r == 2 * j, rows)
    odd = pick(r == 2 * j + 1, rows)
    rim_first = jnp.where(info_ref[3] == 1, 0, -1)
    j_rim = lax.broadcasted_iota(jnp.int32, (count, IDROWS), 0)
    r_rim = lax.broadcasted_iota(jnp.int32, (count, IDROWS), 1)
    before = dot(one((r == 2 * j - 1) & (j != cut)), rows)
    before = before + dot(one((j_rim == rim_first) & (r_rim == IDROWS - 1)), rim_ref[...])
    conv = dot_t(before.astype(jnp.bfloat16), w_conv_ref[0])
    conv = conv + dot_t(even, w_conv_ref[1])
    conv = conv + dot_t(odd, w_conv_ref[2])
    pooled_ref[...] = gelu(conv).astype(jnp.bfloat16)
    piece = count // 4
    turned = [pooled_ref[pl.ds(pl.multiple_of(lax.rem(tp + k, 4) * piece, piece), piece), :] for k in range(4)]
    lm = dot(jnp.concatenate(turned, axis=0), w_proj_ref[...]).astype(jnp.bfloat16)
    for k, out in enumerate((lm0, lm1, lm2, lm3)):
        out[...] = lm[k * piece:(k + 1) * piece]


def lm_sum_kernel(own, got1, got2, got3, out_ref):
    total = own[...].astype(jnp.float32)
    for piece in (got1, got2, got3):
        total = total + piece[...].astype(jnp.float32)
    out_ref[...] = total.astype(jnp.bfloat16)


def params(mib):
    return pltpu.CompilerParams(vmem_limit_bytes=mib << 20)


def cost(flops, moved):
    return pl.CostEstimate(flops=int(flops), bytes_accessed=int(moved), transcendentals=0)


def bf16(*shape):
    return jax.ShapeDtypeStruct(shape, jnp.bfloat16)


def attend(ids, normed, w_qkv, kv):
    rows = normed.shape[0]
    width = w_qkv.shape[1]
    parity = lax.rem(lax.axis_index(SEQ), 2)
    far_back, far_on = send_seq(kv, 4), send_seq(kv, -4)
    back, on = send_seq(kv, 2), send_seq(kv, -2)
    five = send_five(kv)
    beside = send_partner(kv)
    queries = pl.pallas_call(
        query_kernel,
        out_shape=bf16(rows, 384),
        grid=(1,),
        in_specs=[
            pl.BlockSpec(normed.shape, lambda i: (0, 0)),
            pl.BlockSpec((1,) + w_qkv.shape[1:], lambda i: (0, 0, 0)),
        ],
        out_specs=pl.BlockSpec((rows, 384), lambda i: (0, 0)),
        compiler_params=params(16),
        cost_estimate=cost(2e8, 2e6),
    )(normed, w_qkv)
    chain = [far_back, back, kv, on, far_on]
    swapped = [send_partner(far_back), send_partner(back), beside, send_partner(on), send_partner(far_on)]
    info = jnp.concatenate([ids, parity[None].astype(jnp.int32)])
    return pl.pallas_call(
        attend_kernel,
        out_shape=(bf16(rows, width), jax.ShapeDtypeStruct((1,), jnp.int32)),
        in_specs=[SMEM, VMEM] + [ANY] * 11,
        out_specs=(VMEM, SMEM),
        scratch_shapes=[
            pltpu.VMEM((12 * rows, kv.shape[1]), jnp.bfloat16),
            pltpu.VMEM((12, IDROWS, 128), jnp.bfloat16),
            pltpu.SemaphoreType.DMA((11,)),
            pltpu.SemaphoreType.DMA((11,)),
        ],
        compiler_params=params(24),
        cost_estimate=cost(1e9, 4e6),
    )(info, queries, *chain, *swapped, five)


def exchange(parts):
    far = send_tp(parts[1], 2)
    return [send_tp(parts[0], 1), far, send_tp(parts[2], 3)]


def shards(frames, gain_attn, w_qkv, w_out, gain_ffn, w_up, w_down, w_conv, w_proj, block_utt):
    rows, width = frames.shape
    share = rows // 4
    lm_width = w_proj.shape[1]
    w_qkv = jnp.swapaxes(w_qkv, 1, 2)
    w_conv = jnp.swapaxes(w_conv, 1, 2)
    tp = lax.axis_index(TP).astype(jnp.int32)[None]
    w_out_all = lax.all_gather(w_out, TP, tiled=True)
    normed, kv = pl.pallas_call(
        kv_kernel,
        out_shape=(bf16(rows, width), bf16(rows + IDROWS, 2 * w_qkv.shape[1])),
        in_specs=[SMEM, VMEM, VMEM, VMEM],
        out_specs=(VMEM, VMEM),
        compiler_params=params(16),
        cost_estimate=cost(4e8, 4e6),
    )(block_utt, frames, gain_attn[None], w_qkv)
    attended, joined = attend(block_utt, normed, w_qkv, kv)
    heads = exchange([attended] * 3)

    resid, *parts = pl.pallas_call(
        mlp_kernel,
        out_shape=[jax.ShapeDtypeStruct((share + IDROWS, width), jnp.float32)] + [bf16(share + IDROWS, width)] * 4,
        in_specs=[SMEM] + [VMEM] * 9,
        out_specs=[VMEM] * 5,
        scratch_shapes=[pltpu.VMEM((rows, width), jnp.float32), pltpu.VMEM((rows, width), jnp.bfloat16)],
        compiler_params=params(32),
        cost_estimate=cost(2.5e9, 1e7),
    )(tp, attended, *heads, w_out_all, frames, gain_ffn[None], w_up, w_down)
    own, rim = pl.pallas_call(
        layer_sum_kernel,
        out_shape=[bf16(share, width), bf16(IDROWS, width)],
        in_specs=[VMEM] * 5,
        out_specs=[VMEM] * 2,
        compiler_params=params(8),
        cost_estimate=cost(1e6, 1e6),
    )(resid, parts[0], *exchange(parts[1:]))
    layer = exchange([own] * 3)
    rim = send_seq(rim, 1)
    info = jnp.concatenate([tp, block_utt, joined])
    pooled_count = rows // 2
    lm = pl.pallas_call(
        adapter_kernel,
        out_shape=[bf16(pooled_count // 4, lm_width)] * 4,
        in_specs=[SMEM] + [VMEM] * 7,
        out_specs=[VMEM] * 4,
        scratch_shapes=[pltpu.VMEM((rows, width), jnp.bfloat16), pltpu.VMEM((pooled_count, w_conv.shape[1]), jnp.bfloat16)],
        compiler_params=params(24),
        cost_estimate=cost(1e9, 6e6),
    )(info, own, *layer, rim, w_conv, w_proj)
    return pl.pallas_call(
        lm_sum_kernel,
        out_shape=bf16(pooled_count // 4, lm_width),
        in_specs=[VMEM] * 4,
        out_specs=VMEM,
        compiler_params=params(8),
        cost_estimate=cost(1e6, 1e6),
    )(lm[0], *exchange(lm[1:]))


def solution(mesh):
    placed = (
        P("seq", None),
        P(),
        P(None, None, "tp"),
        P("tp", None),
        P(),
        P(None, "tp"),
        P("tp", None),
        P(None, None, "tp"),
        P("tp", None),
        P("seq"),
    )
    return jax.shard_map(
        shards, mesh=mesh, in_specs=placed, out_specs=P(("seq", "tp"), None), check_vma=False
    )
```

```python
import jax
import jax.numpy as jnp
from jax import lax
from jax.experimental import pallas as pl
from jax.experimental.pallas import tpu as pltpu
from jax.sharding import PartitionSpec as P

HEAD_DIM = 64
BLK = 128
MOST = 11
IDROWS = 16
SEQ = "seq"
TP = "tp"
VMEM = pl.BlockSpec(memory_space=pltpu.VMEM)
SMEM = pl.BlockSpec(memory_space=pltpu.SMEM)
ANY = pl.BlockSpec(memory_space=pl.ANY)
HBM = pl.BlockSpec(memory_space=pltpu.HBM)


def send_tp(value, steps):
    count = lax.axis_size(TP)
    return lax.ppermute(value, TP, [(t, (t + steps) % count) for t in range(count)])


def send_seq(value, steps):
    count = lax.axis_size(SEQ)
    return lax.ppermute(
        value, SEQ, [(s, s + steps) for s in range(count) if 0 <= s + steps < count]
    )


def send_partner(value):
    count = lax.axis_size(SEQ)
    return lax.ppermute(value, SEQ, [(s, s ^ 1) for s in range(count)])


def send_five(value):
    count = lax.axis_size(SEQ)
    pairs = [(s, s + 5 if s % 2 else s - 5) for s in range(count)]
    return lax.ppermute(value, SEQ, [(a, b) for a, b in pairs if 0 <= b < count])


def layer_norm(value, gain):
    mean = jnp.mean(value, axis=-1, keepdims=True)
    centred = value - mean
    spread = jnp.mean(centred * centred, axis=-1, keepdims=True)
    return centred * lax.rsqrt(spread + 1e-05) * gain


def dot_t(left, right):
    return lax.dot_general(left, right, (((1,), (1,)), ((), ())), preferred_element_type=jnp.float32)


def dot(left, right):
    return jnp.dot(left, right, preferred_element_type=jnp.float32)


def gelu(value):
    return 0.5 * value * (1.0 + lax.erf(value * (0.5 ** 0.5)))


def kv_kernel(ids_ref, core_ref, tp_ref, frames_hbm, gain_ref, w_hbm, w_out_hbm,
              core_out, tp_out, normed_ref, kv_ref, w_mine_ref,
              frames_ref, w_ref, sems):
    rows = frames_ref.shape[0]
    core_out[0] = core_ref[0]
    tp_out[0] = tp_ref[0]
    copies = [pltpu.make_async_copy(frames_hbm, frames_ref, sems.at[0])]
    copies += [pltpu.make_async_copy(w_hbm.at[k], w_ref.at[k - 1], sems.at[k]) for k in (1, 2)]
    half = w_mine_ref.shape[1]
    copies.append(pltpu.make_async_copy(
        w_out_hbm.at[:, pl.ds(pl.multiple_of(core_ref[0] * half, half), half)], w_mine_ref, sems.at[3]))
    for copy in copies:
        copy.start()
    copies[0].wait()
    normed = layer_norm(frames_ref[...].astype(jnp.float32), gain_ref[...][None]).astype(jnp.bfloat16)
    normed_ref[...] = normed
    copies[1].wait()
    keys = dot_t(normed, w_ref[0]).astype(jnp.bfloat16)
    copies[2].wait()
    values = dot_t(normed, w_ref[1]).astype(jnp.bfloat16)
    kv_ref[:rows, :256] = keys[:, :256]
    kv_ref[:rows, 256:512] = values[:, :256]
    kv_ref[:rows, 512:576] = keys[:, 256:]
    kv_ref[:rows, 576:] = values[:, 256:]
    row = lax.broadcasted_iota(jnp.int32, (IDROWS, kv_ref.shape[1]), 0)
    marks = jnp.where(row == 0, ids_ref[0] + 1, jnp.where(row == 1, ids_ref[1] + 1, 0))
    kv_ref[rows:, :] = marks.astype(jnp.float32).astype(jnp.bfloat16)
    copies[3].wait()


def attend_kernel(ids_ref, core_ref, q_ref, *refs):
    pieces, (out_ref, joined_ref, buf, marks, sems, mark_sems) = refs[:11], refs[11:]
    parity = core_ref[0]
    rows = q_ref.shape[0]
    copies = []
    for n, piece in enumerate(pieces):
        if n < 5:
            slot = 1 + 2 * n + parity
        elif n < 10:
            slot = 2 * (n - 4) - parity
        else:
            slot = 11 * parity
        copies.append(pltpu.make_async_copy(
            piece.at[pl.ds(rows, IDROWS), pl.ds(0, 128)], marks.at[slot], mark_sems.at[n]))
        copies.append(pltpu.make_async_copy(
            piece.at[pl.ds(0, rows), :], buf.at[pl.ds(pl.multiple_of(slot * rows, rows), rows), :], sems.at[n]))
    for copy in copies:
        copy.start()
    unused = 11 - 11 * parity
    marks[unused] = jnp.zeros(marks.shape[1:], marks.dtype)
    for copy in copies:
        copy.wait()
    seen = marks[...].astype(jnp.float32)
    row = lax.broadcasted_iota(jnp.int32, seen.shape, 1)
    place = (2 * lax.broadcasted_iota(jnp.int32, seen.shape, 0) + row).astype(jnp.float32)
    lane = lax.broadcasted_iota(jnp.int32, (BLK, 128), 1)
    column = lax.broadcasted_iota(jnp.int32, (1, MOST * BLK), 1)
    low = lane < HEAD_DIM
    for i in range(2):
        mine = (ids_ref[i] + 1).astype(jnp.float32)
        same = (seen == mine) & (row < 2)
        first = jnp.min(jnp.where(same, place, 99.0)).astype(jnp.int32)
        last = jnp.max(jnp.where(same, place, -1.0)).astype(jnp.int32)
        if i == 0:
            joined_ref[0] = (first < 10 + 2 * parity).astype(jnp.int32)
        start = jnp.clip(first, 2 * parity, MOST + 2 * parity)
        begin = pl.multiple_of(start * BLK, BLK)
        kept = (last + 1 - start) * BLK
        bias = jnp.where(column < kept, 0.0, -1e30)
        window = pl.ds(begin, MOST * BLK)
        for pair in range(3):
            if pair < 2:
                q_pair = q_ref[i * BLK:(i + 1) * BLK, pair * 128:(pair + 1) * 128]
                keys = buf[window, pair * 128:(pair + 1) * 128]
                values = buf[window, 256 + pair * 128:256 + (pair + 1) * 128]
            else:
                q_pair = q_ref[i * BLK:(i + 1) * BLK, 256:384]
                keys = buf[window, 512:640]
                values = keys
            q_pair = q_pair * jnp.asarray(HEAD_DIM ** -0.5, q_pair.dtype)
            halves = []
            for half in range(2 if pair < 2 else 1):
                q_head = jnp.where(low if half == 0 else ~low, q_pair, jnp.zeros_like(q_pair))
                scores = lax.dot_general(
                    q_head, keys, (((1,), (1,)), ((), ())), preferred_element_type=jnp.float32) + bias
                top = jnp.max(scores, axis=-1, keepdims=True)
                weights = jnp.exp(scores - top)
                total = jnp.sum(weights, axis=-1, keepdims=True)
                summed = jnp.dot(weights.astype(jnp.bfloat16), values, preferred_element_type=jnp.float32)
                halves.append(summed / total)
            if pair < 2:
                merged = jnp.where(low, halves[0], halves[1])
                out_ref[i * BLK:(i + 1) * BLK, pair * 128:(pair + 1) * 128] = merged.astype(jnp.bfloat16)
            else:
                out_ref[i * BLK:(i + 1) * BLK, 256:] = halves[0][:, HEAD_DIM:].astype(jnp.bfloat16)


def query_kernel(normed_ref, w_ref, q_ref):
    q_ref[...] = jnp.zeros_like(q_ref)
    q_ref[:, :w_ref.shape[1]] = dot_t(normed_ref[...], w_ref[0]).astype(jnp.bfloat16)


def mlp_kernel(tp_ref, core_ref, att0, att1, att2, att3, w_out_ref, *refs):
    pieces, frames_ref, gain_ref, w_up_ref, w_down_ref = refs[:6], *refs[6:10]
    resid_ref, part0, part1, part2, part3 = refs[10:15]
    resid_all, part_all = refs[15:]
    tp = tp_ref[0]
    rows = att0.shape[0]
    share = rows // 4
    half = pieces[0].shape[1]
    resid_all[...] = frames_ref[...].astype(jnp.float32) + dot(att0[...], w_out_ref[...])
    for n, side in enumerate((core_ref[0], 1 - core_ref[0])):
        columns = pl.ds(pl.multiple_of(side * half, half), half)
        term = resid_all[:, columns]
        for k, att in enumerate((att1, att2, att3)):
            term = term + dot(att[...], pieces[3 * n + k][...])
        resid_all[:, columns] = term
    resid = resid_all[...]
    normed = layer_norm(resid, gain_ref[...][None]).astype(jnp.bfloat16)
    hidden = gelu(dot(normed, w_up_ref[...])).astype(jnp.bfloat16)
    part_all[...] = dot(hidden, w_down_ref[...]).astype(jnp.bfloat16)
    mine = pl.ds(pl.multiple_of(tp * share, share), share)
    resid_ref[:share, :] = resid_all[mine, :]
    resid_ref[share:, :] = resid_all[rows - IDROWS:, :]
    for k, part in enumerate((part0, part1, part2, part3)):
        target = lax.rem(tp + k, 4)
        part[:share, :] = part_all[pl.ds(pl.multiple_of(target * share, share), share), :]
        part[share:, :] = part_all[rows - IDROWS:, :]


def layer_sum_kernel(resid_ref, own, got1, got2, got3, out_ref, rim_ref):
    total = resid_ref[...] + own[...].astype(jnp.float32)
    for piece in (got1, got2, got3):
        total = total + piece[...].astype(jnp.float32)
    share = out_ref.shape[0]
    out_ref[...] = total[:share].astype(jnp.bfloat16)
    rim_ref[...] = total[share:].astype(jnp.bfloat16)


def adapter_kernel(tp_ref, ids_ref, joined_ref, own, got1, got2, got3, rim_ref, w_conv_ref, w_proj_ref,
                   lm0, lm1, lm2, lm3, rows_ref, pooled_ref):
    tp = tp_ref[0]
    share = own.shape[0]
    for k, piece in enumerate((own, got1, got2, got3)):
        source = lax.rem(tp + 4 - k, 4)
        rows_ref[pl.ds(pl.multiple_of(source * share, share), share), :] = piece[...]
    rows = rows_ref[...]
    count = rows.shape[0] // 2
    j = lax.broadcasted_iota(jnp.int32, (count, 2 * count), 0)
    r = lax.broadcasted_iota(jnp.int32, (count, 2 * count), 1)
    same_block = ids_ref[0] == ids_ref[1]
    cut = jnp.where(same_block, -1, count // 2)
    one = lambda flag: jnp.where(flag, 1.0, 0.0).astype(jnp.bfloat16)
    pick = lambda flag, source: dot(one(flag), source).astype(jnp.bfloat16)
    even = pick(r == 2 * j, rows)
    odd = pick(r == 2 * j + 1, rows)
    rim_first = jnp.where(joined_ref[0] == 1, 0, -1)
    j_rim = lax.broadcasted_iota(jnp.int32, (count, IDROWS), 0)
    r_rim = lax.broadcasted_iota(jnp.int32, (count, IDROWS), 1)
    before = dot(one((r == 2 * j - 1) & (j != cut)), rows)
    before = before + dot(one((j_rim == rim_first) & (r_rim == IDROWS - 1)), rim_ref[...])
    conv = dot_t(before.astype(jnp.bfloat16), w_conv_ref[0])
    conv = conv + dot_t(even, w_conv_ref[1])
    conv = conv + dot_t(odd, w_conv_ref[2])
    pooled_ref[...] = gelu(conv).astype(jnp.bfloat16)
    piece = count // 4
    turned = [pooled_ref[pl.ds(pl.multiple_of(lax.rem(tp + k, 4) * piece, piece), piece), :] for k in range(4)]
    lm = dot(jnp.concatenate(turned, axis=0), w_proj_ref[...]).astype(jnp.bfloat16)
    for k, out in enumerate((lm0, lm1, lm2, lm3)):
        out[...] = lm[k * piece:(k + 1) * piece]


def lm_sum_kernel(own, got1, got2, got3, out_ref):
    total = own[...].astype(jnp.float32)
    for piece in (got1, got2, got3):
        total = total + piece[...].astype(jnp.float32)
    out_ref[...] = total.astype(jnp.bfloat16)


def params(mib):
    return pltpu.CompilerParams(vmem_limit_bytes=mib << 20)


def cost(flops, moved):
    return pl.CostEstimate(flops=int(flops), bytes_accessed=int(moved), transcendentals=0)


def bf16(*shape):
    return jax.ShapeDtypeStruct(shape, jnp.bfloat16)


def attend(ids, core, normed, w_qkv, kv, w_mine):
    rows = normed.shape[0]
    width = w_qkv.shape[1]
    back, on = send_seq(kv, 2), send_seq(kv, -2)
    five = send_five(kv)
    w_two = send_tp(w_mine, 2)
    beside = send_partner(kv)
    whole = lambda array: pl.BlockSpec(array.shape, lambda i: (0,) * array.ndim)
    queries = pl.pallas_call(
        query_kernel,
        grid=(1,),
        out_shape=bf16(rows, 384),
        in_specs=[whole(normed), pl.BlockSpec((1,) + w_qkv.shape[1:], lambda i: (0, 0, 0))],
        out_specs=pl.BlockSpec((rows, 384), lambda i: (0, 0)),
        compiler_params=params(4),
        cost_estimate=cost(2e8, 2e6),
    )(normed, w_qkv)
    back, on, five, queries = lax.optimization_barrier((back, on, five, queries))
    far_back, far_on = send_seq(back, 2), send_seq(on, -2)
    w_one, w_three = send_tp(w_mine, 1), send_tp(w_mine, 3)
    far_back, far_on, w_two = lax.optimization_barrier((far_back, far_on, w_two))
    chain = [far_back, back, kv, on, far_on]
    swapped = [send_partner(far_back), send_partner(back), beside, send_partner(on), send_partner(far_on)]
    return pl.pallas_call(
        attend_kernel,
        out_shape=(bf16(rows, width), jax.ShapeDtypeStruct((1,), jnp.int32)),
        in_specs=[SMEM, SMEM, VMEM] + [ANY] * 11,
        out_specs=(VMEM, SMEM),
        scratch_shapes=[
            pltpu.VMEM((12 * rows, kv.shape[1]), jnp.bfloat16),
            pltpu.VMEM((12, IDROWS, 128), jnp.bfloat16),
            pltpu.SemaphoreType.DMA((11,)),
            pltpu.SemaphoreType.DMA((11,)),
        ],
        compiler_params=params(14),
        cost_estimate=cost(1e9, 4e6),
    )(ids, core, queries, *chain, *swapped, five), [w_one, w_two, w_three]


def exchange(parts):
    far = send_tp(parts[1], 2)
    return [send_tp(parts[0], 1), far, send_tp(parts[2], 3)]


def shards(frames, gain_attn, w_qkv, w_out, gain_ffn, w_up, w_down, w_conv, w_proj, block_utt):
    rows, width = frames.shape
    share = rows // 4
    lm_width = w_proj.shape[1]
    w_qkv = jnp.swapaxes(w_qkv, 1, 2)
    w_conv = jnp.swapaxes(w_conv, 1, 2)
    tp = lax.axis_index(TP).astype(jnp.int32)[None]
    core = lax.rem(lax.axis_index(SEQ), 2).astype(jnp.int32)[None]
    scalar = jax.ShapeDtypeStruct((1,), jnp.int32)
    core, tp, normed, kv, w_mine = pl.pallas_call(
        kv_kernel,
        out_shape=(scalar, scalar, bf16(rows, width), bf16(rows + IDROWS, 2 * w_qkv.shape[1]), bf16(w_out.shape[0], width // 2)),
        in_specs=[SMEM, SMEM, SMEM, HBM, VMEM, HBM, HBM],
        out_specs=(SMEM, SMEM, VMEM, VMEM, VMEM),
        scratch_shapes=[
            pltpu.VMEM((rows, width), jnp.bfloat16),
            pltpu.VMEM((2,) + w_qkv.shape[1:], jnp.bfloat16),
            pltpu.SemaphoreType.DMA((4,)),
        ],
        compiler_params=params(60),
        cost_estimate=cost(4e8, 4e6),
    )(block_utt, core, tp, frames, gain_attn, w_qkv, w_out)
    (attended, joined), w_mine = attend(block_utt, core, normed, w_qkv, kv, w_mine)
    attended, *w_mine = lax.optimization_barrier((attended, *w_mine))
    w_other = [send_partner(piece) for piece in w_mine]
    heads = exchange([attended] * 3)

    resid, *parts = pl.pallas_call(
        mlp_kernel,
        out_shape=[jax.ShapeDtypeStruct((share + IDROWS, width), jnp.float32)] + [bf16(share + IDROWS, width)] * 4,
        in_specs=[SMEM] * 2 + [VMEM] * 15,
        out_specs=[VMEM] * 5,
        scratch_shapes=[pltpu.VMEM((rows, width), jnp.float32), pltpu.VMEM((rows, width), jnp.bfloat16)],
        compiler_params=params(14),
        cost_estimate=cost(2.5e9, 1e7),
    )(tp, core, attended, *heads, w_out, *w_mine, *w_other, frames, gain_ffn, w_up, w_down)
    own, rim = pl.pallas_call(
        layer_sum_kernel,
        out_shape=[bf16(share, width), bf16(IDROWS, width)],
        in_specs=[VMEM] * 5,
        out_specs=[VMEM] * 2,
        compiler_params=params(4),
        cost_estimate=cost(1e6, 1e6),
    )(resid, parts[0], *exchange(parts[1:]))
    layer = exchange([own] * 3)
    rim = send_seq(rim, 1)
    pooled_count = rows // 2
    lm = pl.pallas_call(
        adapter_kernel,
        out_shape=[bf16(pooled_count // 4, lm_width)] * 4,
        in_specs=[SMEM] * 3 + [VMEM] * 7,
        out_specs=[VMEM] * 4,
        scratch_shapes=[pltpu.VMEM((rows, width), jnp.bfloat16), pltpu.VMEM((pooled_count, w_conv.shape[1]), jnp.bfloat16)],
        compiler_params=params(10),
        cost_estimate=cost(1e9, 6e6),
    )(tp, block_utt, joined, own, *layer, rim, w_conv, w_proj)
    return pl.pallas_call(
        lm_sum_kernel,
        out_shape=bf16(pooled_count // 4, lm_width),
        in_specs=[VMEM] * 4,
        out_specs=VMEM,
        compiler_params=params(4),
        cost_estimate=cost(1e6, 1e6),
    )(lm[0], *exchange(lm[1:]))


def solution(mesh):
    placed = (
        P("seq", None),
        P(),
        P(None, None, "tp"),
        P("tp", None),
        P(),
        P(None, "tp"),
        P("tp", None),
        P(None, None, "tp"),
        P("tp", None),
        P("seq"),
    )
    return jax.shard_map(
        shards, mesh=mesh, in_specs=placed, out_specs=P(("seq", "tp"), None), check_vma=False
    )
```

```python
import jax
import jax.numpy as jnp
from jax import lax
from jax.experimental import pallas as pl
from jax.experimental.pallas import tpu as pltpu
from jax.sharding import PartitionSpec as P

HEAD_DIM = 64
BLK = 128
MOST = 11
IDROWS = 16
SEQ = "seq"
TP = "tp"
VMEM = pl.BlockSpec(memory_space=pltpu.VMEM)
SMEM = pl.BlockSpec(memory_space=pltpu.SMEM)
ANY = pl.BlockSpec(memory_space=pl.ANY)
HBM = pl.BlockSpec(memory_space=pltpu.HBM)


def send_tp(value, steps):
    count = lax.axis_size(TP)
    return lax.ppermute(value, TP, [(t, (t + steps) % count) for t in range(count)])


def send_seq(value, steps):
    count = lax.axis_size(SEQ)
    return lax.ppermute(
        value, SEQ, [(s, s + steps) for s in range(count) if 0 <= s + steps < count]
    )


def send_partner(value):
    count = lax.axis_size(SEQ)
    return lax.ppermute(value, SEQ, [(s, s ^ 1) for s in range(count)])


def send_five(value):
    count = lax.axis_size(SEQ)
    pairs = [(s, s + 5 if s % 2 else s - 5) for s in range(count)]
    return lax.ppermute(value, SEQ, [(a, b) for a, b in pairs if 0 <= b < count])


def layer_norm(value, gain):
    mean = jnp.mean(value, axis=-1, keepdims=True)
    centred = value - mean
    spread = jnp.mean(centred * centred, axis=-1, keepdims=True)
    return centred * lax.rsqrt(spread + 1e-05) * gain


def dot_t(left, right):
    return lax.dot_general(left, right, (((1,), (1,)), ((), ())), preferred_element_type=jnp.float32)


def dot(left, right):
    return jnp.dot(left, right, preferred_element_type=jnp.float32)


def gelu(value):
    return 0.5 * value * (1.0 + lax.erf(value * (0.5 ** 0.5)))


def kv_kernel(ids_ref, core_ref, tp_ref, frames_hbm, gain_ref, w_hbm, w_out_hbm,
              core_out, tp_out, normed_ref, kv_ref, w_mine_ref,
              frames_ref, w_ref, sems):
    rows = frames_ref.shape[0]
    core_out[0] = core_ref[0]
    tp_out[0] = tp_ref[0]
    copies = [pltpu.make_async_copy(frames_hbm, frames_ref, sems.at[0])]
    copies += [pltpu.make_async_copy(w_hbm.at[k], w_ref.at[k - 1], sems.at[k]) for k in (1, 2)]
    half = w_mine_ref.shape[1]
    copies.append(pltpu.make_async_copy(
        w_out_hbm.at[:, pl.ds(pl.multiple_of(core_ref[0] * half, half), half)], w_mine_ref, sems.at[3]))
    for copy in copies:
        copy.start()
    copies[0].wait()
    normed = layer_norm(frames_ref[...].astype(jnp.float32), gain_ref[...][None]).astype(jnp.bfloat16)
    normed_ref[...] = normed
    copies[1].wait()
    keys = dot_t(normed, w_ref[0]).astype(jnp.bfloat16)
    copies[2].wait()
    values = dot_t(normed, w_ref[1]).astype(jnp.bfloat16)
    kv_ref[:rows, :256] = keys[:, :256]
    kv_ref[:rows, 256:512] = values[:, :256]
    kv_ref[:rows, 512:576] = keys[:, 256:]
    kv_ref[:rows, 576:] = values[:, 256:]
    row = lax.broadcasted_iota(jnp.int32, (IDROWS, kv_ref.shape[1]), 0)
    marks = jnp.where(row == 0, ids_ref[0] + 1, jnp.where(row == 1, ids_ref[1] + 1, 0))
    kv_ref[rows:, :] = marks.astype(jnp.float32).astype(jnp.bfloat16)
    copies[3].wait()


def attend_kernel(ids_ref, core_ref, q_ref, *refs):
    pieces, (out_ref, joined_ref, buf, marks, sems, mark_sems) = refs[:11], refs[11:]
    parity = core_ref[0]
    rows = q_ref.shape[0]
    copies = []
    for n, piece in enumerate(pieces):
        if n < 5:
            slot = 1 + 2 * n + parity
        elif n < 10:
            slot = 2 * (n - 4) - parity
        else:
            slot = 11 * parity
        copies.append(pltpu.make_async_copy(
            piece.at[pl.ds(rows, IDROWS), pl.ds(0, 128)], marks.at[slot], mark_sems.at[n]))
        copies.append(pltpu.make_async_copy(
            piece.at[pl.ds(0, rows), :], buf.at[pl.ds(pl.multiple_of(slot * rows, rows), rows), :], sems.at[n]))
    for copy in copies:
        copy.start()
    unused = 11 - 11 * parity
    marks[unused] = jnp.zeros(marks.shape[1:], marks.dtype)
    for copy in copies:
        copy.wait()
    seen = marks[...].astype(jnp.float32)
    row = lax.broadcasted_iota(jnp.int32, seen.shape, 1)
    place = (2 * lax.broadcasted_iota(jnp.int32, seen.shape, 0) + row).astype(jnp.float32)
    lane = lax.broadcasted_iota(jnp.int32, (BLK, 128), 1)
    column = lax.broadcasted_iota(jnp.int32, (1, MOST * BLK), 1)
    low = lane < HEAD_DIM
    for i in range(2):
        mine = (ids_ref[i] + 1).astype(jnp.float32)
        same = (seen == mine) & (row < 2)
        first = jnp.min(jnp.where(same, place, 99.0)).astype(jnp.int32)
        last = jnp.max(jnp.where(same, place, -1.0)).astype(jnp.int32)
        if i == 0:
            joined_ref[0] = (first < 10 + 2 * parity).astype(jnp.int32)
        start = jnp.clip(first, 2 * parity, MOST + 2 * parity)
        begin = pl.multiple_of(start * BLK, BLK)
        kept = (last + 1 - start) * BLK
        bias = jnp.where(column < kept, 0.0, -1e30)
        window = pl.ds(begin, MOST * BLK)
        for pair in range(3):
            q_pair = q_ref[i * BLK:(i + 1) * BLK, pair * 128:(pair + 1) * 128]
            q_pair = q_pair * jnp.asarray(HEAD_DIM ** -0.5, q_pair.dtype)
            none = jnp.zeros_like(q_pair)
            key_at, value_at = ((0, 256), (128, 384), (512, 512))[pair]
            q_both = jnp.where(low, q_pair, none)
            if pair < 2:
                q_both = jnp.concatenate([q_both, jnp.where(low, none, q_pair)], axis=0)
            scores = dot_t(q_both, buf[window, key_at:key_at + 128]) + bias
            top = jnp.max(scores, axis=-1, keepdims=True)
            weights = jnp.exp(scores - top)
            total = jnp.sum(weights, axis=-1, keepdims=True)
            summed = dot(weights.astype(jnp.bfloat16), buf[window, value_at:value_at + 128]) / total
            if pair < 2:
                merged = jnp.where(low, summed[:BLK], summed[BLK:])
                out_ref[i * BLK:(i + 1) * BLK, pair * 128:(pair + 1) * 128] = merged.astype(jnp.bfloat16)
            else:
                out_ref[i * BLK:(i + 1) * BLK, 256:] = summed[:, HEAD_DIM:].astype(jnp.bfloat16)


def query_kernel(normed_ref, w_ref, kv_in, w_down_in, q_ref, kv_ref, w_down_ref):
    q_ref[...] = jnp.zeros_like(q_ref)
    q_ref[:, :w_ref.shape[1]] = dot_t(normed_ref[...], w_ref[0]).astype(jnp.bfloat16)
    kv_ref[...] = kv_in[...]
    w_down_ref[...] = w_down_in[...]


def mlp_kernel(tp_ref, core_ref, att0, att1, att2, att3, w_out_ref, *refs):
    pieces, frames_ref, gain_ref, w_up_ref, w_down_ref = refs[:6], *refs[6:10]
    resid_ref, part0, part1, part2, part3 = refs[10:15]
    resid_all, part_all = refs[15:]
    tp = tp_ref[0]
    rows = att0.shape[0]
    share = rows // 4
    half = pieces[0].shape[1]
    resid_all[...] = frames_ref[...].astype(jnp.float32) + dot(att0[...], w_out_ref[...])
    for n, side in enumerate((core_ref[0], 1 - core_ref[0])):
        columns = pl.ds(pl.multiple_of(side * half, half), half)
        term = resid_all[:, columns]
        for k, att in enumerate((att1, att2, att3)):
            term = term + dot(att[...], pieces[3 * n + k][...])
        resid_all[:, columns] = term
    resid = resid_all[...]
    normed = layer_norm(resid, gain_ref[...][None]).astype(jnp.bfloat16)
    hidden = gelu(dot(normed, w_up_ref[...])).astype(jnp.bfloat16)
    part_all[...] = dot(hidden, w_down_ref[...]).astype(jnp.bfloat16)
    mine = pl.ds(pl.multiple_of(tp * share, share), share)
    resid_ref[:share, :] = resid_all[mine, :]
    resid_ref[share:, :] = resid_all[rows - IDROWS:, :]
    for k, part in enumerate((part0, part1, part2, part3)):
        target = lax.rem(tp + k, 4)
        part[:share, :] = part_all[pl.ds(pl.multiple_of(target * share, share), share), :]
        part[share:, :] = part_all[rows - IDROWS:, :]


def layer_sum_kernel(resid_ref, own, got1, got2, got3, out_ref, rim_ref):
    total = resid_ref[...] + own[...].astype(jnp.float32)
    for piece in (got1, got2, got3):
        total = total + piece[...].astype(jnp.float32)
    share = out_ref.shape[0]
    out_ref[...] = total[:share].astype(jnp.bfloat16)
    rim_ref[...] = total[share:].astype(jnp.bfloat16)


def adapter_kernel(tp_ref, ids_ref, joined_ref, own, got1, got2, got3, rim_ref, w_conv_ref, w_proj_ref,
                   lm0, lm1, lm2, lm3, rows_ref, pooled_ref):
    tp = tp_ref[0]
    share = own.shape[0]
    for k, piece in enumerate((own, got1, got2, got3)):
        source = lax.rem(tp + 4 - k, 4)
        rows_ref[pl.ds(pl.multiple_of(source * share, share), share), :] = piece[...]
    rows = rows_ref[...]
    count = rows.shape[0] // 2
    j = lax.broadcasted_iota(jnp.int32, (count, 2 * count), 0)
    r = lax.broadcasted_iota(jnp.int32, (count, 2 * count), 1)
    same_block = ids_ref[0] == ids_ref[1]
    cut = jnp.where(same_block, -1, count // 2)
    one = lambda flag: jnp.where(flag, 1.0, 0.0).astype(jnp.bfloat16)
    pick = lambda flag, source: dot(one(flag), source).astype(jnp.bfloat16)
    even = pick(r == 2 * j, rows)
    odd = pick(r == 2 * j + 1, rows)
    rim_first = jnp.where(joined_ref[0] == 1, 0, -1)
    j_rim = lax.broadcasted_iota(jnp.int32, (count, IDROWS), 0)
    r_rim = lax.broadcasted_iota(jnp.int32, (count, IDROWS), 1)
    before = dot(one((r == 2 * j - 1) & (j != cut)), rows)
    before = before + dot(one((j_rim == rim_first) & (r_rim == IDROWS - 1)), rim_ref[...])
    conv = dot_t(before.astype(jnp.bfloat16), w_conv_ref[0])
    conv = conv + dot_t(even, w_conv_ref[1])
    conv = conv + dot_t(odd, w_conv_ref[2])
    pooled_ref[...] = gelu(conv).astype(jnp.bfloat16)
    piece = count // 4
    turned = [pooled_ref[pl.ds(pl.multiple_of(lax.rem(tp + k, 4) * piece, piece), piece), :] for k in range(4)]
    lm = dot(jnp.concatenate(turned, axis=0), w_proj_ref[...]).astype(jnp.bfloat16)
    for k, out in enumerate((lm0, lm1, lm2, lm3)):
        out[...] = lm[k * piece:(k + 1) * piece]


def lm_sum_kernel(own, got1, got2, got3, out_ref):
    total = own[...].astype(jnp.float32)
    for piece in (got1, got2, got3):
        total = total + piece[...].astype(jnp.float32)
    out_ref[...] = total.astype(jnp.bfloat16)


def params(mib):
    return pltpu.CompilerParams(vmem_limit_bytes=mib << 20)


def cost(flops, moved):
    return pl.CostEstimate(flops=int(flops), bytes_accessed=int(moved), transcendentals=0)


def bf16(*shape):
    return jax.ShapeDtypeStruct(shape, jnp.bfloat16)


def attend(ids, core, normed, w_qkv, kv, w_mine, w_down):
    rows = normed.shape[0]
    width = w_qkv.shape[1]
    back, on = send_seq(kv, 2), send_seq(kv, -2)
    w_two = send_tp(w_mine, 2)
    beside = send_partner(kv)
    whole = lambda array: pl.BlockSpec(array.shape, lambda i: (0,) * array.ndim)
    queries, kv_held, w_down = pl.pallas_call(
        query_kernel,
        grid=(1,),
        out_shape=[bf16(rows, 384), bf16(*kv.shape), bf16(*w_down.shape)],
        in_specs=[whole(normed), pl.BlockSpec((1,) + w_qkv.shape[1:], lambda i: (0, 0, 0)), VMEM, VMEM],
        out_specs=[pl.BlockSpec((rows, 384), lambda i: (0, 0)), VMEM, VMEM],
        compiler_params=params(4),
        cost_estimate=cost(2e8, 2e6),
    )(normed, w_qkv, kv, w_down)
    back, on, queries, kv_late = lax.optimization_barrier((back, on, queries, kv))
    five = send_five(kv_late)
    far_back, far_on = send_seq(back, 2), send_seq(on, -2)
    w_one, w_three = send_tp(w_mine, 1), send_tp(w_mine, 3)
    far_back, far_on, w_two, w_one, five = lax.optimization_barrier((far_back, far_on, w_two, w_one, five))
    chain = [far_back, back, kv_held, on, far_on]
    swapped = [send_partner(far_back), send_partner(back), beside, send_partner(on), send_partner(far_on)]
    return pl.pallas_call(
        attend_kernel,
        out_shape=(bf16(rows, width), jax.ShapeDtypeStruct((1,), jnp.int32)),
        in_specs=[SMEM, SMEM, VMEM] + [ANY] * 11,
        out_specs=(VMEM, SMEM),
        scratch_shapes=[
            pltpu.VMEM((12 * rows, kv.shape[1]), jnp.bfloat16),
            pltpu.VMEM((12, IDROWS, 128), jnp.bfloat16),
            pltpu.SemaphoreType.DMA((11,)),
            pltpu.SemaphoreType.DMA((11,)),
        ],
        compiler_params=params(14),
        cost_estimate=cost(1e9, 4e6),
    )(ids, core, queries, *chain, *swapped, five), [w_one, w_two, w_three], w_down


def exchange(parts):
    far = send_tp(parts[1], 2)
    return [send_tp(parts[0], 1), far, send_tp(parts[2], 3)]


def shards(frames, gain_attn, w_qkv, w_out, gain_ffn, w_up, w_down, w_conv, w_proj, block_utt):
    rows, width = frames.shape
    share = rows // 4
    lm_width = w_proj.shape[1]
    w_qkv = jnp.swapaxes(w_qkv, 1, 2)
    w_conv = jnp.swapaxes(w_conv, 1, 2)
    tp = lax.axis_index(TP).astype(jnp.int32)[None]
    core = lax.rem(lax.axis_index(SEQ), 2).astype(jnp.int32)[None]
    scalar = jax.ShapeDtypeStruct((1,), jnp.int32)
    core, tp, normed, kv, w_mine = pl.pallas_call(
        kv_kernel,
        out_shape=(scalar, scalar, bf16(rows, width), bf16(rows + IDROWS, 2 * w_qkv.shape[1]), bf16(w_out.shape[0], width // 2)),
        in_specs=[SMEM, SMEM, SMEM, HBM, VMEM, HBM, HBM],
        out_specs=(SMEM, SMEM, VMEM, VMEM, VMEM),
        scratch_shapes=[
            pltpu.VMEM((rows, width), jnp.bfloat16),
            pltpu.VMEM((2,) + w_qkv.shape[1:], jnp.bfloat16),
            pltpu.SemaphoreType.DMA((4,)),
        ],
        compiler_params=params(60),
        cost_estimate=cost(4e8, 4e6),
    )(block_utt, core, tp, frames, gain_attn, w_qkv, w_out)
    (attended, joined), w_mine, w_down = attend(block_utt, core, normed, w_qkv, kv, w_mine, w_down)
    w_other = [send_partner(piece) for piece in w_mine]
    attended, *w_other = lax.optimization_barrier((attended, *w_other))
    heads = exchange([attended] * 3)

    resid, *parts = pl.pallas_call(
        mlp_kernel,
        out_shape=[jax.ShapeDtypeStruct((share + IDROWS, width), jnp.float32)] + [bf16(share + IDROWS, width)] * 4,
        in_specs=[SMEM] * 2 + [VMEM] * 15,
        out_specs=[VMEM] * 5,
        scratch_shapes=[pltpu.VMEM((rows, width), jnp.float32), pltpu.VMEM((rows, width), jnp.bfloat16)],
        compiler_params=params(14),
        cost_estimate=cost(2.5e9, 1e7),
    )(tp, core, attended, *heads, w_out, *w_mine, *w_other, frames, gain_ffn, w_up, w_down)
    own, rim = pl.pallas_call(
        layer_sum_kernel,
        out_shape=[bf16(share, width), bf16(IDROWS, width)],
        in_specs=[VMEM] * 5,
        out_specs=[VMEM] * 2,
        compiler_params=params(4),
        cost_estimate=cost(1e6, 1e6),
    )(resid, parts[0], *exchange(parts[1:]))
    layer = exchange([own] * 3)
    rim = send_seq(rim, 1)
    pooled_count = rows // 2
    lm = pl.pallas_call(
        adapter_kernel,
        out_shape=[bf16(pooled_count // 4, lm_width)] * 4,
        in_specs=[SMEM] * 3 + [VMEM] * 7,
        out_specs=[VMEM] * 4,
        scratch_shapes=[pltpu.VMEM((rows, width), jnp.bfloat16), pltpu.VMEM((pooled_count, w_conv.shape[1]), jnp.bfloat16)],
        compiler_params=params(10),
        cost_estimate=cost(1e9, 6e6),
    )(tp, block_utt, joined, own, *layer, rim, w_conv, w_proj)
    return pl.pallas_call(
        lm_sum_kernel,
        out_shape=bf16(pooled_count // 4, lm_width),
        in_specs=[VMEM] * 4,
        out_specs=VMEM,
        compiler_params=params(4),
        cost_estimate=cost(1e6, 1e6),
    )(lm[0], *exchange(lm[1:]))


def solution(mesh):
    placed = (
        P("seq", None),
        P(),
        P(None, None, "tp"),
        P("tp", None),
        P(),
        P(None, "tp"),
        P("tp", None),
        P(None, None, "tp"),
        P("tp", None),
        P("seq"),
    )
    return jax.shard_map(
        shards, mesh=mesh, in_specs=placed, out_specs=P(("seq", "tp"), None), check_vma=False
    )
```

```python
import jax
import jax.numpy as jnp
from jax import lax
from jax.experimental import pallas as pl
from jax.experimental.pallas import tpu as pltpu
from jax.sharding import PartitionSpec as P

HEAD_DIM = 64
BLK = 128
MOST = 11
IDROWS = 16
SEQ = "seq"
TP = "tp"
VMEM = pl.BlockSpec(memory_space=pltpu.VMEM)
SMEM = pl.BlockSpec(memory_space=pltpu.SMEM)
ANY = pl.BlockSpec(memory_space=pl.ANY)
HBM = pl.BlockSpec(memory_space=pltpu.HBM)


def send_tp(value, steps):
    count = lax.axis_size(TP)
    return lax.ppermute(value, TP, [(t, (t + steps) % count) for t in range(count)])


def send_seq(value, steps):
    count = lax.axis_size(SEQ)
    return lax.ppermute(
        value, SEQ, [(s, s + steps) for s in range(count) if 0 <= s + steps < count]
    )


def send_chip(value, turn):
    count = lax.axis_size(SEQ)
    pairs = [(s, s + 2 * turn * (1 if s % 2 else -1)) for s in range(count)]
    return lax.ppermute(value, SEQ, [(a, b) for a, b in pairs if 0 <= b < count])


def send_partner(value):
    count = lax.axis_size(SEQ)
    return lax.ppermute(value, SEQ, [(s, s ^ 1) for s in range(count)])


def send_five(value):
    count = lax.axis_size(SEQ)
    pairs = [(s, s + 5 if s % 2 else s - 5) for s in range(count)]
    return lax.ppermute(value, SEQ, [(a, b) for a, b in pairs if 0 <= b < count])


def layer_norm(value, gain):
    mean = jnp.mean(value, axis=-1, keepdims=True)
    centred = value - mean
    spread = jnp.mean(centred * centred, axis=-1, keepdims=True)
    return centred * lax.rsqrt(spread + 1e-05) * gain


def dot_t(left, right):
    return lax.dot_general(left, right, (((1,), (1,)), ((), ())), preferred_element_type=jnp.float32)


def dot(left, right):
    return jnp.dot(left, right, preferred_element_type=jnp.float32)


def gelu(value):
    return 0.5 * value * (1.0 + lax.erf(value * (0.5 ** 0.5)))


def kv_kernel(ids_ref, core_ref, tp_ref, frames_hbm, gain_ref, w_hbm, w_out_hbm,
              core_out, tp_out, normed_ref, kv_ref, w_mine_ref,
              frames_ref, w_ref, sems):
    rows = frames_ref.shape[0]
    core_out[0] = core_ref[0]
    tp_out[0] = tp_ref[0]
    copies = [pltpu.make_async_copy(frames_hbm, frames_ref, sems.at[0])]
    copies += [pltpu.make_async_copy(w_hbm.at[k], w_ref.at[k - 1], sems.at[k]) for k in (1, 2)]
    half = w_mine_ref.shape[1]
    copies.append(pltpu.make_async_copy(
        w_out_hbm.at[:, pl.ds(pl.multiple_of(core_ref[0] * half, half), half)], w_mine_ref, sems.at[3]))
    for copy in copies:
        copy.start()
    copies[0].wait()
    normed = layer_norm(frames_ref[...].astype(jnp.float32), gain_ref[...][None]).astype(jnp.bfloat16)
    normed_ref[...] = normed
    copies[1].wait()
    keys = dot_t(normed, w_ref[0]).astype(jnp.bfloat16)
    copies[2].wait()
    values = dot_t(normed, w_ref[1]).astype(jnp.bfloat16)
    kv_ref[:rows, :256] = keys[:, :256]
    kv_ref[:rows, 256:512] = values[:, :256]
    kv_ref[:rows, 512:576] = keys[:, 256:]
    kv_ref[:rows, 576:] = values[:, 256:]
    row = lax.broadcasted_iota(jnp.int32, (IDROWS, kv_ref.shape[1]), 0)
    marks = jnp.where(row == 0, ids_ref[0] + 1, jnp.where(row == 1, ids_ref[1] + 1, 0))
    kv_ref[rows:, :] = marks.astype(jnp.float32).astype(jnp.bfloat16)
    copies[3].wait()


def attend_kernel(ids_ref, core_ref, q_ref, *refs):
    pieces, (out_ref, joined_ref, buf, marks, sems, mark_sems) = refs[:11], refs[11:]
    parity = core_ref[0]
    rows = q_ref.shape[0]
    copies = []
    for n, piece in enumerate(pieces):
        slot = (9 - 7 * parity, 7 - 3 * parity, 5 + parity, 3 + 5 * parity, 1 + 9 * parity,
                2 + 7 * parity, 4 + 3 * parity, 6 - parity, 8 - 5 * parity, 10 - 9 * parity, 11 * parity)[n]
        copies.append(pltpu.make_async_copy(
            piece.at[pl.ds(rows, IDROWS), pl.ds(0, 128)], marks.at[slot], mark_sems.at[n]))
        copies.append(pltpu.make_async_copy(
            piece.at[pl.ds(0, rows), :], buf.at[pl.ds(pl.multiple_of(slot * rows, rows), rows), :], sems.at[n]))
    for copy in copies:
        copy.start()
    unused = 11 - 11 * parity
    marks[unused] = jnp.zeros(marks.shape[1:], marks.dtype)
    for copy in copies:
        copy.wait()
    seen = marks[...].astype(jnp.float32)
    row = lax.broadcasted_iota(jnp.int32, seen.shape, 1)
    place = (2 * lax.broadcasted_iota(jnp.int32, seen.shape, 0) + row).astype(jnp.float32)
    lane = lax.broadcasted_iota(jnp.int32, (BLK, 128), 1)
    column = lax.broadcasted_iota(jnp.int32, (1, MOST * BLK), 1)
    low = lane < HEAD_DIM
    for i in range(2):
        mine = (ids_ref[i] + 1).astype(jnp.float32)
        same = (seen == mine) & (row < 2)
        first = jnp.min(jnp.where(same, place, 99.0)).astype(jnp.int32)
        last = jnp.max(jnp.where(same, place, -1.0)).astype(jnp.int32)
        if i == 0:
            joined_ref[0] = (first < 10 + 2 * parity).astype(jnp.int32)
        start = jnp.clip(first, 2 * parity, MOST + 2 * parity)
        begin = pl.multiple_of(start * BLK, BLK)
        kept = (last + 1 - start) * BLK
        bias = jnp.where(column < kept, 0.0, -1e30)
        window = pl.ds(begin, MOST * BLK)
        for pair in range(3):
            q_pair = q_ref[i * BLK:(i + 1) * BLK, pair * 128:(pair + 1) * 128]
            q_pair = q_pair * jnp.asarray(HEAD_DIM ** -0.5, q_pair.dtype)
            none = jnp.zeros_like(q_pair)
            key_at, value_at = ((0, 256), (128, 384), (512, 512))[pair]
            q_both = jnp.where(low, q_pair, none)
            if pair < 2:
                q_both = jnp.concatenate([q_both, jnp.where(low, none, q_pair)], axis=0)
            scores = dot_t(q_both, buf[window, key_at:key_at + 128]) + bias
            top = jnp.max(scores, axis=-1, keepdims=True)
            weights = jnp.exp(scores - top)
            total = jnp.sum(weights, axis=-1, keepdims=True)
            summed = dot(weights.astype(jnp.bfloat16), buf[window, value_at:value_at + 128]) / total
            if pair < 2:
                merged = jnp.where(low, summed[:BLK], summed[BLK:])
                out_ref[i * BLK:(i + 1) * BLK, pair * 128:(pair + 1) * 128] = merged.astype(jnp.bfloat16)
            else:
                out_ref[i * BLK:(i + 1) * BLK, 256:] = summed[:, HEAD_DIM:].astype(jnp.bfloat16)


def query_kernel(normed_ref, w_ref, kv_in, w_down_in, q_ref, kv_ref, w_down_ref):
    q_ref[...] = jnp.zeros_like(q_ref)
    q_ref[:, :w_ref.shape[1]] = dot_t(normed_ref[...], w_ref[0]).astype(jnp.bfloat16)
    kv_ref[...] = kv_in[...]
    w_down_ref[...] = w_down_in[...]


def last_row(ref):
    rows, width = ref.shape
    row = ref[rows - 8:, :][7:8]
    pieces = [row[:, g * 128:(g + 1) * 128] for g in range(width // 128)]
    pieces.append(jnp.zeros((IDROWS - len(pieces), 128), row.dtype))
    return jnp.concatenate(pieces, axis=0)


def mlp_kernel(tp_ref, core_ref, att0, att1, att2, att3, w_out_ref, *refs):
    pieces, frames_ref, gain_ref, w_up_ref, w_down_ref = refs[:6], *refs[6:10]
    resid_ref, part0, part1, part2, part3 = refs[10:15]
    resid_all, part_all = refs[15:]
    tp = tp_ref[0]
    rows = att0.shape[0]
    share = rows // 4
    half = pieces[0].shape[1]
    resid_all[...] = frames_ref[...].astype(jnp.float32) + dot(att0[...], w_out_ref[...])
    for n, side in enumerate((core_ref[0], 1 - core_ref[0])):
        columns = pl.ds(pl.multiple_of(side * half, half), half)
        term = resid_all[:, columns]
        for k, att in enumerate((att1, att2, att3)):
            term = term + dot(att[...], pieces[3 * n + k][...])
        resid_all[:, columns] = term
    resid = resid_all[...]
    normed = layer_norm(resid, gain_ref[...][None]).astype(jnp.bfloat16)
    hidden = gelu(dot(normed, w_up_ref[...])).astype(jnp.bfloat16)
    part_all[...] = dot(hidden, w_down_ref[...])
    mine = pl.ds(pl.multiple_of(tp * share, share), share)
    groups = resid_all.shape[1] // 128
    resid_ref[groups * share:, :] = last_row(resid_all)
    last = last_row(part_all).astype(jnp.bfloat16)
    for g in range(groups):
        resid_ref[g * share:(g + 1) * share, :] = resid_all[mine, g * 128:(g + 1) * 128]
    for k, part in enumerate((part0, part1, part2, part3)):
        target = pl.ds(pl.multiple_of(lax.rem(tp + k, 4) * share, share), share)
        for g in range(groups):
            part[g * share:(g + 1) * share, :] = part_all[target, g * 128:(g + 1) * 128].astype(jnp.bfloat16)
        part[groups * share:, :] = last


def layer_sum_kernel(resid_ref, own, got1, got2, got3, out_ref, rim_ref):
    total = resid_ref[...] + own[...].astype(jnp.float32)
    for piece in (got1, got2, got3):
        total = total + piece[...].astype(jnp.float32)
    share, width = out_ref.shape
    groups = width // 128
    for g in range(groups):
        out_ref[:, g * 128:(g + 1) * 128] = total[g * share:(g + 1) * share].astype(jnp.bfloat16)
    rim_ref[...] = total[groups * share:].astype(jnp.bfloat16)


def adapter_kernel(tp_ref, ids_ref, joined_ref, own, got1, got2, got3, rim_ref, w_conv_ref, w_proj_ref,
                   lm0, lm1, lm2, lm3, rows_ref, pooled_ref):
    tp = tp_ref[0]
    share = own.shape[0]
    for k, piece in enumerate((own, got1, got2, got3)):
        source = lax.rem(tp + 4 - k, 4)
        rows_ref[pl.ds(pl.multiple_of(source * share, share), share), :] = piece[...]
    rows = rows_ref[...]
    count = rows.shape[0] // 2
    j = lax.broadcasted_iota(jnp.int32, (count, 2 * count), 0)
    r = lax.broadcasted_iota(jnp.int32, (count, 2 * count), 1)
    same_block = ids_ref[0] == ids_ref[1]
    cut = jnp.where(same_block, -1, count // 2)
    one = lambda flag: jnp.where(flag, 1.0, 0.0).astype(jnp.bfloat16)
    pick = lambda flag, source: dot(one(flag), source).astype(jnp.bfloat16)
    even = pick(r == 2 * j, rows)
    odd = pick(r == 2 * j + 1, rows)
    before = dot(one((r == 2 * j - 1) & (j != cut)), rows)
    rim = rim_ref[...].astype(jnp.float32)
    rim = jnp.concatenate([rim[g:g + 1] for g in range(before.shape[1] // 128)], axis=1)
    rim_first = jnp.where(joined_ref[0] == 1, 0, -1)
    top_row = lax.broadcasted_iota(jnp.int32, before.shape, 0) == rim_first
    before = before + jnp.where(top_row, rim, 0.0)
    conv = dot_t(before.astype(jnp.bfloat16), w_conv_ref[0])
    conv = conv + dot_t(even, w_conv_ref[1])
    conv = conv + dot_t(odd, w_conv_ref[2])
    pooled_ref[...] = gelu(conv).astype(jnp.bfloat16)
    piece = count // 4
    turned = [pooled_ref[pl.ds(pl.multiple_of(lax.rem(tp + k, 4) * piece, piece), piece), :] for k in range(4)]
    lm = dot(jnp.concatenate(turned, axis=0), w_proj_ref[...]).astype(jnp.bfloat16)
    for k, out in enumerate((lm0, lm1, lm2, lm3)):
        out[...] = lm[k * piece:(k + 1) * piece]


def lm_sum_kernel(own, got1, got2, got3, out_ref):
    total = own[...].astype(jnp.float32)
    for piece in (got1, got2, got3):
        total = total + piece[...].astype(jnp.float32)
    out_ref[...] = total.astype(jnp.bfloat16)


def params(mib):
    return pltpu.CompilerParams(vmem_limit_bytes=mib << 20)


def cost(flops, moved):
    return pl.CostEstimate(flops=int(flops), bytes_accessed=int(moved), transcendentals=0)


def bf16(*shape):
    return jax.ShapeDtypeStruct(shape, jnp.bfloat16)


def attend(ids, core, normed, w_qkv, kv, w_mine, w_down):
    rows = normed.shape[0]
    width = w_qkv.shape[1]
    back, on = send_chip(kv, 1), send_chip(kv, -1)
    w_two = send_tp(w_mine, 2)
    whole = lambda array: pl.BlockSpec(array.shape, lambda i: (0,) * array.ndim)
    queries, kv_held, w_down = pl.pallas_call(
        query_kernel,
        grid=(1,),
        out_shape=[bf16(rows, 384), bf16(*kv.shape), bf16(*w_down.shape)],
        in_specs=[whole(normed), pl.BlockSpec((1,) + w_qkv.shape[1:], lambda i: (0, 0, 0)), VMEM, VMEM],
        out_specs=[pl.BlockSpec((rows, 384), lambda i: (0, 0)), VMEM, VMEM],
        compiler_params=params(4),
        cost_estimate=cost(2e8, 2e6),
    )(normed, w_qkv, kv, w_down)
    back, kv_late = lax.optimization_barrier((back, kv))
    five = send_five(kv_late)
    far_back, far_on = send_chip(back, 1), send_chip(on, -1)
    w_one, w_three = send_tp(w_mine, 1), send_tp(w_mine, 3)
    far_back, far_on, w_two, w_one, five = lax.optimization_barrier((far_back, far_on, w_two, w_one, five))
    back_again, on_again, kv_again, queries = lax.optimization_barrier((back, on, kv_held, queries))
    beside = send_partner(kv_again)
    chain = [far_back, back, kv_held, on, far_on]
    swapped = [send_partner(far_back), send_partner(back_again), beside, send_partner(on_again), send_partner(far_on)]
    return pl.pallas_call(
        attend_kernel,
        out_shape=(bf16(rows, width), jax.ShapeDtypeStruct((1,), jnp.int32)),
        in_specs=[SMEM, SMEM, VMEM] + [ANY] * 11,
        out_specs=(VMEM, SMEM),
        scratch_shapes=[
            pltpu.VMEM((12 * rows, kv.shape[1]), jnp.bfloat16),
            pltpu.VMEM((12, IDROWS, 128), jnp.bfloat16),
            pltpu.SemaphoreType.DMA((11,)),
            pltpu.SemaphoreType.DMA((11,)),
        ],
        compiler_params=params(14),
        cost_estimate=cost(1e9, 4e6),
    )(ids, core, queries, *chain, *swapped, five), [w_one, w_two, w_three], w_down


def exchange(parts):
    far = send_tp(parts[1], 2)
    return [send_tp(parts[0], 1), far, send_tp(parts[2], 3)]


def shards(frames, gain_attn, w_qkv, w_out, gain_ffn, w_up, w_down, w_conv, w_proj, block_utt):
    rows, width = frames.shape
    share = rows // 4
    lm_width = w_proj.shape[1]
    w_qkv = jnp.swapaxes(w_qkv, 1, 2)
    w_conv = jnp.swapaxes(w_conv, 1, 2)
    tp = lax.axis_index(TP).astype(jnp.int32)[None]
    core = lax.rem(lax.axis_index(SEQ), 2).astype(jnp.int32)[None]
    scalar = jax.ShapeDtypeStruct((1,), jnp.int32)
    core, tp, normed, kv, w_mine = pl.pallas_call(
        kv_kernel,
        out_shape=(scalar, scalar, bf16(rows, width), bf16(rows + IDROWS, 2 * w_qkv.shape[1]), bf16(w_out.shape[0], width // 2)),
        in_specs=[SMEM, SMEM, SMEM, HBM, VMEM, HBM, HBM],
        out_specs=(SMEM, SMEM, VMEM, VMEM, VMEM),
        scratch_shapes=[
            pltpu.VMEM((rows, width), jnp.bfloat16),
            pltpu.VMEM((2,) + w_qkv.shape[1:], jnp.bfloat16),
            pltpu.SemaphoreType.DMA((4,)),
        ],
        compiler_params=params(56),
        cost_estimate=cost(4e8, 4e6),
    )(block_utt, core, tp, frames, gain_attn, w_qkv, w_out)
    (attended, joined), w_mine, w_down = attend(block_utt, core, normed, w_qkv, kv, w_mine, w_down)
    w_other = [send_partner(piece) for piece in w_mine]
    attended, *w_other = lax.optimization_barrier((attended, *w_other))
    heads = exchange([attended] * 3)

    tall = share * (width // 128) + IDROWS
    resid, *parts = pl.pallas_call(
        mlp_kernel,
        out_shape=[jax.ShapeDtypeStruct((tall, 128), jnp.float32)] + [bf16(tall, 128)] * 4,
        in_specs=[SMEM] * 2 + [VMEM] * 15,
        out_specs=[VMEM] * 5,
        scratch_shapes=[pltpu.VMEM((rows, width), jnp.float32)] * 2,
        compiler_params=params(14),
        cost_estimate=cost(2.5e9, 1e7),
    )(tp, core, attended, *heads, w_out, *w_mine, *w_other, frames, gain_ffn, w_up, w_down)
    own, rim = pl.pallas_call(
        layer_sum_kernel,
        out_shape=[bf16(share, width), bf16(IDROWS, 128)],
        in_specs=[VMEM] * 5,
        out_specs=[VMEM] * 2,
        compiler_params=params(4),
        cost_estimate=cost(1e6, 1e6),
    )(resid, parts[0], *exchange(parts[1:]))
    layer = exchange([own] * 3)
    rim = send_seq(rim, 1)
    pooled_count = rows // 2
    lm = pl.pallas_call(
        adapter_kernel,
        out_shape=[bf16(pooled_count // 4, lm_width)] * 4,
        in_specs=[SMEM] * 3 + [VMEM] * 7,
        out_specs=[VMEM] * 4,
        scratch_shapes=[pltpu.VMEM((rows, width), jnp.bfloat16), pltpu.VMEM((pooled_count, w_conv.shape[1]), jnp.bfloat16)],
        compiler_params=params(10),
        cost_estimate=cost(1e9, 6e6),
    )(tp, block_utt, joined, own, *layer, rim, w_conv, w_proj)
    return pl.pallas_call(
        lm_sum_kernel,
        out_shape=bf16(pooled_count // 4, lm_width),
        in_specs=[VMEM] * 4,
        out_specs=VMEM,
        compiler_params=params(4),
        cost_estimate=cost(1e6, 1e6),
    )(lm[0], *exchange(lm[1:]))


def solution(mesh):
    placed = (
        P("seq", None),
        P(),
        P(None, None, "tp"),
        P("tp", None),
        P(),
        P(None, "tp"),
        P("tp", None),
        P(None, None, "tp"),
        P("tp", None),
        P("seq"),
    )
    return jax.shard_map(
        shards, mesh=mesh, in_specs=placed, out_specs=P(("seq", "tp"), None), check_vma=False
    )
```

```python
import jax
import jax.numpy as jnp
from jax import lax
from jax.experimental import pallas as pl
from jax.experimental.pallas import tpu as pltpu
from jax.sharding import PartitionSpec as P

HEAD_DIM = 64
BLK = 128
MOST = 11
IDROWS = 16
SEQ = "seq"
TP = "tp"
VMEM = pl.BlockSpec(memory_space=pltpu.VMEM)
SMEM = pl.BlockSpec(memory_space=pltpu.SMEM)
ANY = pl.BlockSpec(memory_space=pl.ANY)
HBM = pl.BlockSpec(memory_space=pltpu.HBM)


def send_tp(value, steps):
    count = lax.axis_size(TP)
    return lax.ppermute(value, TP, [(t, (t + steps) % count) for t in range(count)])


def send_pair(value, turn):
    seq, count = lax.axis_size(SEQ), lax.axis_size(TP)
    pairs = [(s * count + t, s * count + (t + turn * (-1 if s % 2 else 1)) % count) for s in range(seq) for t in range(count)]
    return lax.ppermute(value, (SEQ, TP), pairs)


def send_seq(value, steps):
    count = lax.axis_size(SEQ)
    return lax.ppermute(
        value, SEQ, [(s, s + steps) for s in range(count) if 0 <= s + steps < count]
    )


def send_chip(value, turn):
    count = lax.axis_size(SEQ)
    pairs = [(s, s + 2 * turn * (1 if s % 2 else -1)) for s in range(count)]
    return lax.ppermute(value, SEQ, [(a, b) for a, b in pairs if 0 <= b < count])


def send_partner(value):
    count = lax.axis_size(SEQ)
    return lax.ppermute(value, SEQ, [(s, s ^ 1) for s in range(count)])


def send_five(value):
    count = lax.axis_size(SEQ)
    pairs = [(s, s + 5 if s % 2 else s - 5) for s in range(count)]
    return lax.ppermute(value, SEQ, [(a, b) for a, b in pairs if 0 <= b < count])


def layer_norm(value, gain):
    mean = jnp.mean(value, axis=-1, keepdims=True)
    centred = value - mean
    spread = jnp.mean(centred * centred, axis=-1, keepdims=True)
    return centred * lax.rsqrt(spread + 1e-05) * gain


def dot_t(left, right):
    return lax.dot_general(left, right, (((1,), (1,)), ((), ())), preferred_element_type=jnp.float32)


def dot(left, right):
    return jnp.dot(left, right, preferred_element_type=jnp.float32)


def gelu(value):
    return 0.5 * value * (1.0 + lax.erf(value * (0.5 ** 0.5)))


def kv_kernel(ids_ref, core_ref, tp_ref, frames_hbm, gain_ref, w_hbm, w_out_hbm,
              core_out, tp_out, normed_ref, kv_ref, w_mine_ref,
              frames_ref, w_ref, sems):
    rows = frames_ref.shape[0]
    core_out[0] = core_ref[0]
    tp_out[0] = tp_ref[0]
    copies = [pltpu.make_async_copy(frames_hbm, frames_ref, sems.at[0])]
    copies += [pltpu.make_async_copy(w_hbm.at[k], w_ref.at[k - 1], sems.at[k]) for k in (1, 2)]
    half = w_mine_ref.shape[1]
    copies.append(pltpu.make_async_copy(
        w_out_hbm.at[:, pl.ds(pl.multiple_of(core_ref[0] * half, half), half)], w_mine_ref, sems.at[3]))
    for copy in copies:
        copy.start()
    copies[0].wait()
    normed = layer_norm(frames_ref[...].astype(jnp.float32), gain_ref[...][None]).astype(jnp.bfloat16)
    normed_ref[...] = normed
    copies[1].wait()
    keys = dot_t(normed, w_ref[0]).astype(jnp.bfloat16)
    copies[2].wait()
    values = dot_t(normed, w_ref[1]).astype(jnp.bfloat16)
    kv_ref[:rows, :256] = keys[:, :256]
    kv_ref[:rows, 256:512] = values[:, :256]
    kv_ref[:rows, 512:576] = keys[:, 256:]
    kv_ref[:rows, 576:] = values[:, 256:]
    row = lax.broadcasted_iota(jnp.int32, (IDROWS, kv_ref.shape[1]), 0)
    marks = jnp.where(row == 0, ids_ref[0] + 1, jnp.where(row == 1, ids_ref[1] + 1, 0))
    kv_ref[rows:, :] = marks.astype(jnp.float32).astype(jnp.bfloat16)
    copies[3].wait()


def attend_kernel(ids_ref, core_ref, q_ref, *refs):
    pieces, (out_ref, joined_ref, buf, marks, sems, mark_sems) = refs[:11], refs[11:]
    parity = core_ref[0]
    rows = q_ref.shape[0]
    copies = []
    for n, piece in enumerate(pieces):
        slot = (9 - 7 * parity, 7 - 3 * parity, 5 + parity, 3 + 5 * parity, 1 + 9 * parity,
                2 + 7 * parity, 4 + 3 * parity, 6 - parity, 8 - 5 * parity, 10 - 9 * parity, 11 * parity)[n]
        copies.append(pltpu.make_async_copy(
            piece.at[pl.ds(rows, IDROWS), pl.ds(0, 128)], marks.at[slot], mark_sems.at[n]))
        copies.append(pltpu.make_async_copy(
            piece.at[pl.ds(0, rows), :], buf.at[pl.ds(pl.multiple_of(slot * rows, rows), rows), :], sems.at[n]))
    for copy in copies:
        copy.start()
    unused = 11 - 11 * parity
    marks[unused] = jnp.zeros(marks.shape[1:], marks.dtype)
    for copy in copies:
        copy.wait()
    seen = marks[...].astype(jnp.float32)
    row = lax.broadcasted_iota(jnp.int32, seen.shape, 1)
    place = (2 * lax.broadcasted_iota(jnp.int32, seen.shape, 0) + row).astype(jnp.float32)
    lane = lax.broadcasted_iota(jnp.int32, (BLK, 128), 1)
    column = lax.broadcasted_iota(jnp.int32, (1, MOST * BLK), 1)
    low = lane < HEAD_DIM
    for i in range(2):
        mine = (ids_ref[i] + 1).astype(jnp.float32)
        same = (seen == mine) & (row < 2)
        first = jnp.min(jnp.where(same, place, 99.0)).astype(jnp.int32)
        last = jnp.max(jnp.where(same, place, -1.0)).astype(jnp.int32)
        if i == 0:
            joined_ref[0] = (first < 10 + 2 * parity).astype(jnp.int32)
        start = jnp.clip(first, 2 * parity, MOST + 2 * parity)
        begin = pl.multiple_of(start * BLK, BLK)
        kept = (last + 1 - start) * BLK
        bias = jnp.where(column < kept, 0.0, -1e30)
        window = pl.ds(begin, MOST * BLK)
        for pair in range(3):
            q_pair = q_ref[i * BLK:(i + 1) * BLK, pair * 128:(pair + 1) * 128]
            q_pair = q_pair * jnp.asarray(HEAD_DIM ** -0.5, q_pair.dtype)
            none = jnp.zeros_like(q_pair)
            key_at, value_at = ((0, 256), (128, 384), (512, 512))[pair]
            q_both = jnp.where(low, q_pair, none)
            if pair < 2:
                q_both = jnp.concatenate([q_both, jnp.where(low, none, q_pair)], axis=0)
            scores = dot_t(q_both, buf[window, key_at:key_at + 128]) + bias
            top = jnp.max(scores, axis=-1, keepdims=True)
            weights = jnp.exp(scores - top)
            total = jnp.sum(weights, axis=-1, keepdims=True)
            summed = dot(weights.astype(jnp.bfloat16), buf[window, value_at:value_at + 128]) / total
            if pair < 2:
                merged = jnp.where(low, summed[:BLK], summed[BLK:])
                out_ref[i * BLK:(i + 1) * BLK, pair * 128:(pair + 1) * 128] = merged.astype(jnp.bfloat16)
            else:
                out_ref[i * BLK:(i + 1) * BLK, 256:] = summed[:, HEAD_DIM:].astype(jnp.bfloat16)


def query_kernel(normed_ref, w_ref, kv_in, w_down_in, q_ref, kv_ref, w_down_ref):
    q_ref[...] = jnp.zeros_like(q_ref)
    q_ref[:, :w_ref.shape[1]] = dot_t(normed_ref[...], w_ref[0]).astype(jnp.bfloat16)
    kv_ref[...] = kv_in[...]
    w_down_ref[...] = w_down_in[...]


def last_row(ref):
    rows, width = ref.shape
    row = ref[rows - 8:, :][7:8]
    pieces = [row[:, g * 128:(g + 1) * 128] for g in range(width // 128)]
    pieces.append(jnp.zeros((IDROWS - len(pieces), 128), row.dtype))
    return jnp.concatenate(pieces, axis=0)


def mlp_kernel(tp_ref, core_ref, att0, att1, att2, att3, w_out_ref, *refs):
    pieces, frames_ref, gain_ref, w_up_ref, w_down_ref = refs[:6], *refs[6:10]
    resid_ref, part0, part1, part2, part3 = refs[10:15]
    resid_all, part_all = refs[15:]
    tp = tp_ref[0]
    rows = att0.shape[0]
    share = rows // 4
    half = pieces[0].shape[1]
    resid_all[...] = frames_ref[...].astype(jnp.float32) + dot(att0[...], w_out_ref[...])
    for n, side in enumerate((core_ref[0], 1 - core_ref[0])):
        columns = pl.ds(pl.multiple_of(side * half, half), half)
        term = resid_all[:, columns]
        for k, att in enumerate((att1, att2, att3)):
            term = term + dot(att[...], pieces[3 * n + k][...])
        resid_all[:, columns] = term
    resid = resid_all[...]
    normed = layer_norm(resid, gain_ref[...][None]).astype(jnp.bfloat16)
    hidden = gelu(dot(normed, w_up_ref[...])).astype(jnp.bfloat16)
    part_all[...] = dot(hidden, w_down_ref[...])
    mine = pl.ds(pl.multiple_of(tp * share, share), share)
    groups = resid_all.shape[1] // 128
    resid_ref[groups * share:, :] = last_row(resid_all)
    last = last_row(part_all).astype(jnp.bfloat16)
    for g in range(groups):
        resid_ref[g * share:(g + 1) * share, :] = resid_all[mine, g * 128:(g + 1) * 128]
    for k, part in enumerate((part0, part1, part2, part3)):
        target = pl.ds(pl.multiple_of(lax.rem(tp + k, 4) * share, share), share)
        for g in range(groups):
            part[g * share:(g + 1) * share, :] = part_all[target, g * 128:(g + 1) * 128].astype(jnp.bfloat16)
        part[groups * share:, :] = last


def layer_sum_kernel(resid_ref, own, got1, got2, got3, out_ref, rim_ref):
    total = resid_ref[...] + own[...].astype(jnp.float32)
    for piece in (got1, got2, got3):
        total = total + piece[...].astype(jnp.float32)
    share, width = out_ref.shape
    groups = width // 128
    for g in range(groups):
        out_ref[:, g * 128:(g + 1) * 128] = total[g * share:(g + 1) * share].astype(jnp.bfloat16)
    rim_ref[...] = total[groups * share:].astype(jnp.bfloat16)


def adapter_kernel(tp_ref, ids_ref, joined_ref, own, got1, got2, got3, rim_ref, w_conv_ref, w_proj_ref,
                   lm0, lm1, lm2, lm3, rows_ref, pooled_ref):
    tp = tp_ref[0]
    share = own.shape[0]
    for k, piece in enumerate((own, got1, got2, got3)):
        source = lax.rem(tp + 4 - k, 4)
        rows_ref[pl.ds(pl.multiple_of(source * share, share), share), :] = piece[...]
    rows = rows_ref[...]
    count = rows.shape[0] // 2
    j = lax.broadcasted_iota(jnp.int32, (count, 2 * count), 0)
    r = lax.broadcasted_iota(jnp.int32, (count, 2 * count), 1)
    same_block = ids_ref[0] == ids_ref[1]
    cut = jnp.where(same_block, -1, count // 2)
    one = lambda flag: jnp.where(flag, 1.0, 0.0).astype(jnp.bfloat16)
    pick = lambda flag, source: dot(one(flag), source).astype(jnp.bfloat16)
    even = pick(r == 2 * j, rows)
    odd = pick(r == 2 * j + 1, rows)
    before = dot(one((r == 2 * j - 1) & (j != cut)), rows)
    rim = rim_ref[...].astype(jnp.float32)
    rim = jnp.concatenate([rim[g:g + 1] for g in range(before.shape[1] // 128)], axis=1)
    rim_first = jnp.where(joined_ref[0] == 1, 0, -1)
    top_row = lax.broadcasted_iota(jnp.int32, before.shape, 0) == rim_first
    before = before + jnp.where(top_row, rim, 0.0)
    conv = dot_t(before.astype(jnp.bfloat16), w_conv_ref[0])
    conv = conv + dot_t(even, w_conv_ref[1])
    conv = conv + dot_t(odd, w_conv_ref[2])
    pooled_ref[...] = gelu(conv).astype(jnp.bfloat16)
    piece = count // 4
    turned = [pooled_ref[pl.ds(pl.multiple_of(lax.rem(tp + k, 4) * piece, piece), piece), :] for k in range(4)]
    lm = dot(jnp.concatenate(turned, axis=0), w_proj_ref[...]).astype(jnp.bfloat16)
    for k, out in enumerate((lm0, lm1, lm2, lm3)):
        out[...] = lm[k * piece:(k + 1) * piece]


def lm_sum_kernel(own, got1, got2, got3, out_ref):
    total = own[...].astype(jnp.float32)
    for piece in (got1, got2, got3):
        total = total + piece[...].astype(jnp.float32)
    out_ref[...] = total.astype(jnp.bfloat16)


def params(mib):
    return pltpu.CompilerParams(vmem_limit_bytes=mib << 20)


def cost(flops, moved):
    return pl.CostEstimate(flops=int(flops), bytes_accessed=int(moved), transcendentals=0)


def bf16(*shape):
    return jax.ShapeDtypeStruct(shape, jnp.bfloat16)


def attend(ids, core, normed, w_qkv, kv, w_mine, w_down):
    rows = normed.shape[0]
    width = w_qkv.shape[1]
    back, on = send_chip(kv, 1), send_chip(kv, -1)
    w_two = send_tp(w_mine, 2)
    whole = lambda array: pl.BlockSpec(array.shape, lambda i: (0,) * array.ndim)
    queries, kv_held, w_down = pl.pallas_call(
        query_kernel,
        grid=(1,),
        out_shape=[bf16(rows, 384), bf16(*kv.shape), bf16(*w_down.shape)],
        in_specs=[whole(normed), pl.BlockSpec((1,) + w_qkv.shape[1:], lambda i: (0, 0, 0)), VMEM, VMEM],
        out_specs=[pl.BlockSpec((rows, 384), lambda i: (0, 0)), VMEM, VMEM],
        compiler_params=params(4),
        cost_estimate=cost(2e8, 2e6),
    )(normed, w_qkv, kv, w_down)
    back, kv_late = lax.optimization_barrier((back, kv))
    five = send_five(kv_late)
    far_back, far_on = send_chip(back, 1), send_chip(on, -1)
    w_one, w_three = send_pair(w_mine, 1), send_pair(w_mine, -1)
    far_back, far_on, w_two, w_one, five = lax.optimization_barrier((far_back, far_on, w_two, w_one, five))
    back_again, on_again, kv_again, queries = lax.optimization_barrier((back, on, kv_held, queries))
    beside = send_partner(kv_again)
    chain = [far_back, back, kv_held, on, far_on]
    swapped = [send_partner(far_back), send_partner(back_again), beside, send_partner(on_again), send_partner(far_on)]
    return pl.pallas_call(
        attend_kernel,
        out_shape=(bf16(rows, width), jax.ShapeDtypeStruct((1,), jnp.int32)),
        in_specs=[SMEM, SMEM, VMEM] + [ANY] * 11,
        out_specs=(VMEM, SMEM),
        scratch_shapes=[
            pltpu.VMEM((12 * rows, kv.shape[1]), jnp.bfloat16),
            pltpu.VMEM((12, IDROWS, 128), jnp.bfloat16),
            pltpu.SemaphoreType.DMA((11,)),
            pltpu.SemaphoreType.DMA((11,)),
        ],
        compiler_params=params(14),
        cost_estimate=cost(1e9, 4e6),
    )(ids, core, queries, *chain, *swapped, five), [w_one, w_two, w_three], w_down


def exchange(parts):
    far = send_tp(parts[1], 2)
    return [send_tp(parts[0], 1), far, send_tp(parts[2], 3)]


def shards(frames, gain_attn, w_qkv, w_out, gain_ffn, w_up, w_down, w_conv, w_proj, block_utt):
    rows, width = frames.shape
    share = rows // 4
    lm_width = w_proj.shape[1]
    w_qkv = jnp.swapaxes(w_qkv, 1, 2)
    w_conv = jnp.swapaxes(w_conv, 1, 2)
    tp = lax.axis_index(TP).astype(jnp.int32)[None]
    core = lax.rem(lax.axis_index(SEQ), 2).astype(jnp.int32)[None]
    scalar = jax.ShapeDtypeStruct((1,), jnp.int32)
    core, tp, normed, kv, w_mine = pl.pallas_call(
        kv_kernel,
        out_shape=(scalar, scalar, bf16(rows, width), bf16(rows + IDROWS, 2 * w_qkv.shape[1]), bf16(w_out.shape[0], width // 2)),
        in_specs=[SMEM, SMEM, SMEM, HBM, VMEM, HBM, HBM],
        out_specs=(SMEM, SMEM, VMEM, VMEM, VMEM),
        scratch_shapes=[
            pltpu.VMEM((rows, width), jnp.bfloat16),
            pltpu.VMEM((2,) + w_qkv.shape[1:], jnp.bfloat16),
            pltpu.SemaphoreType.DMA((4,)),
        ],
        compiler_params=params(56),
        cost_estimate=cost(4e8, 4e6),
    )(block_utt, core, tp, frames, gain_attn, w_qkv, w_out)
    (attended, joined), w_mine, w_down = attend(block_utt, core, normed, w_qkv, kv, w_mine, w_down)
    w_other = [send_partner(piece) for piece in reversed(w_mine)]
    attended, *w_other = lax.optimization_barrier((attended, *w_other))
    heads = [send_pair(attended, 1), send_tp(attended, 2), send_pair(attended, -1)]

    tall = share * (width // 128) + IDROWS
    resid, *parts = pl.pallas_call(
        mlp_kernel,
        out_shape=[jax.ShapeDtypeStruct((tall, 128), jnp.float32)] + [bf16(tall, 128)] * 4,
        in_specs=[SMEM] * 2 + [VMEM] * 15,
        out_specs=[VMEM] * 5,
        scratch_shapes=[pltpu.VMEM((rows, width), jnp.float32)] * 2,
        compiler_params=params(14),
        cost_estimate=cost(2.5e9, 1e7),
    )(tp, core, attended, *heads, w_out, *w_mine, *w_other, frames, gain_ffn, w_up, w_down)
    own, rim = pl.pallas_call(
        layer_sum_kernel,
        out_shape=[bf16(share, width), bf16(IDROWS, 128)],
        in_specs=[VMEM] * 5,
        out_specs=[VMEM] * 2,
        compiler_params=params(4),
        cost_estimate=cost(1e6, 1e6),
    )(resid, parts[0], *exchange(parts[1:]))
    layer = exchange([own] * 3)
    rim = send_seq(rim, 1)
    pooled_count = rows // 2
    lm = pl.pallas_call(
        adapter_kernel,
        out_shape=[bf16(pooled_count // 4, lm_width)] * 4,
        in_specs=[SMEM] * 3 + [VMEM] * 7,
        out_specs=[VMEM] * 4,
        scratch_shapes=[pltpu.VMEM((rows, width), jnp.bfloat16), pltpu.VMEM((pooled_count, w_conv.shape[1]), jnp.bfloat16)],
        compiler_params=params(10),
        cost_estimate=cost(1e9, 6e6),
    )(tp, block_utt, joined, own, *layer, rim, w_conv, w_proj)
    return pl.pallas_call(
        lm_sum_kernel,
        out_shape=bf16(pooled_count // 4, lm_width),
        in_specs=[VMEM] * 4,
        out_specs=VMEM,
        compiler_params=params(4),
        cost_estimate=cost(1e6, 1e6),
    )(lm[0], *exchange(lm[1:]))


def solution(mesh):
    placed = (
        P("seq", None),
        P(),
        P(None, None, "tp"),
        P("tp", None),
        P(),
        P(None, "tp"),
        P("tp", None),
        P(None, None, "tp"),
        P("tp", None),
        P("seq"),
    )
    return jax.shard_map(
        shards, mesh=mesh, in_specs=placed, out_specs=P(("seq", "tp"), None), check_vma=False
    )
```

```python
import jax
import jax.numpy as jnp
from jax import lax
from jax.experimental import pallas as pl
from jax.experimental.pallas import tpu as pltpu
from jax.sharding import PartitionSpec as P

HEAD_DIM = 64
BLK = 128
MOST = 11
IDROWS = 16
SEQ = "seq"
TP = "tp"
VMEM = pl.BlockSpec(memory_space=pltpu.VMEM)
SMEM = pl.BlockSpec(memory_space=pltpu.SMEM)
ANY = pl.BlockSpec(memory_space=pl.ANY)
HBM = pl.BlockSpec(memory_space=pltpu.HBM)


def send_tp(value, steps):
    count = lax.axis_size(TP)
    return lax.ppermute(value, TP, [(t, (t + steps) % count) for t in range(count)])


def send_pair(value, turn):
    seq, count = lax.axis_size(SEQ), lax.axis_size(TP)
    pairs = [(s * count + t, s * count + (t + turn * (-1 if s % 2 else 1)) % count) for s in range(seq) for t in range(count)]
    return lax.ppermute(value, (SEQ, TP), pairs)


def send_seq(value, steps):
    count = lax.axis_size(SEQ)
    return lax.ppermute(
        value, SEQ, [(s, s + steps) for s in range(count) if 0 <= s + steps < count]
    )


def send_chip(value, turn):
    count = lax.axis_size(SEQ)
    pairs = [(s, s + 2 * turn * (1 if s % 2 else -1)) for s in range(count)]
    return lax.ppermute(value, SEQ, [(a, b) for a, b in pairs if 0 <= b < count])


def send_partner(value):
    count = lax.axis_size(SEQ)
    return lax.ppermute(value, SEQ, [(s, s ^ 1) for s in range(count)])


def send_five(value):
    count = lax.axis_size(SEQ)
    pairs = [(s, s + 5 if s % 2 else s - 5) for s in range(count)]
    return lax.ppermute(value, SEQ, [(a, b) for a, b in pairs if 0 <= b < count])


def layer_norm(value, gain):
    mean = jnp.mean(value, axis=-1, keepdims=True)
    centred = value - mean
    spread = jnp.mean(centred * centred, axis=-1, keepdims=True)
    return centred * lax.rsqrt(spread + 1e-05) * gain


def dot_t(left, right):
    return lax.dot_general(left, right, (((1,), (1,)), ((), ())), preferred_element_type=jnp.float32)


def dot(left, right):
    return jnp.dot(left, right, preferred_element_type=jnp.float32)


def gelu(value):
    return 0.5 * value * (1.0 + lax.erf(value * (0.5 ** 0.5)))


def kv_kernel(ids_ref, core_ref, tp_ref, frames_hbm, gain_ref, w_hbm, w_out_hbm,
              core_out, tp_out, normed_out, kv_ref, w_mine_ref,
              frames_ref, w_ref, normed_ref, sems):
    rows = frames_ref.shape[0]
    core_out[0] = core_ref[0]
    tp_out[0] = tp_ref[0]
    copies = [pltpu.make_async_copy(frames_hbm, frames_ref, sems.at[0])]
    copies += [pltpu.make_async_copy(w_hbm.at[k], w_ref.at[k - 1], sems.at[k]) for k in (1, 2)]
    half = w_mine_ref.shape[1]
    copies.append(pltpu.make_async_copy(
        w_out_hbm.at[:, pl.ds(pl.multiple_of(core_ref[0] * half, half), half)], w_mine_ref, sems.at[3]))
    for copy in copies:
        copy.start()
    copies[0].wait()
    normed = layer_norm(frames_ref[...].astype(jnp.float32), gain_ref[...][None]).astype(jnp.bfloat16)
    normed_ref[...] = normed
    copies.append(pltpu.make_async_copy(normed_ref, normed_out, sems.at[4]))
    copies[4].start()
    copies[1].wait()
    keys = dot_t(normed, w_ref[0]).astype(jnp.bfloat16)
    copies[2].wait()
    values = dot_t(normed, w_ref[1]).astype(jnp.bfloat16)
    kv_ref[:rows, :256] = keys[:, :256]
    kv_ref[:rows, 256:512] = values[:, :256]
    kv_ref[:rows, 512:576] = keys[:, 256:]
    kv_ref[:rows, 576:] = values[:, 256:]
    row = lax.broadcasted_iota(jnp.int32, (IDROWS, kv_ref.shape[1]), 0)
    marks = jnp.where(row == 0, ids_ref[0] + 1, jnp.where(row == 1, ids_ref[1] + 1, 0))
    kv_ref[rows:, :] = marks.astype(jnp.float32).astype(jnp.bfloat16)
    copies[3].wait()
    copies[4].wait()


def attend_kernel(ids_ref, core_ref, q_ref, *refs):
    pieces, (out_ref, joined_ref, buf, marks, sems, mark_sems) = refs[:11], refs[11:]
    parity = core_ref[0]
    rows = q_ref.shape[0]
    copies = []
    for n, piece in enumerate(pieces):
        slot = (9 - 7 * parity, 7 - 3 * parity, 5 + parity, 3 + 5 * parity, 1 + 9 * parity,
                2 + 7 * parity, 4 + 3 * parity, 6 - parity, 8 - 5 * parity, 10 - 9 * parity, 11 * parity)[n]
        copies.append(pltpu.make_async_copy(
            piece.at[pl.ds(rows, IDROWS), pl.ds(0, 128)], marks.at[slot], mark_sems.at[n]))
        copies.append(pltpu.make_async_copy(
            piece.at[pl.ds(0, rows), :], buf.at[pl.ds(pl.multiple_of(slot * rows, rows), rows), :], sems.at[n]))
    for copy in copies:
        copy.start()
    unused = 11 - 11 * parity
    marks[unused] = jnp.zeros(marks.shape[1:], marks.dtype)
    for copy in copies:
        copy.wait()
    seen = marks[...].astype(jnp.float32)
    row = lax.broadcasted_iota(jnp.int32, seen.shape, 1)
    place = (2 * lax.broadcasted_iota(jnp.int32, seen.shape, 0) + row).astype(jnp.float32)
    lane = lax.broadcasted_iota(jnp.int32, (BLK, 128), 1)
    column = lax.broadcasted_iota(jnp.int32, (1, MOST * BLK), 1)
    low = lane < HEAD_DIM
    for i in range(2):
        mine = (ids_ref[i] + 1).astype(jnp.float32)
        same = (seen == mine) & (row < 2)
        first = jnp.min(jnp.where(same, place, 99.0)).astype(jnp.int32)
        last = jnp.max(jnp.where(same, place, -1.0)).astype(jnp.int32)
        if i == 0:
            joined_ref[0] = (first < 10 + 2 * parity).astype(jnp.int32)
        start = jnp.clip(first, 2 * parity, MOST + 2 * parity)
        begin = pl.multiple_of(start * BLK, BLK)
        kept = (last + 1 - start) * BLK
        bias = jnp.where(column < kept, 0.0, -1e30)
        window = pl.ds(begin, MOST * BLK)
        for pair in range(3):
            q_pair = q_ref[i * BLK:(i + 1) * BLK, pair * 128:(pair + 1) * 128]
            q_pair = q_pair * jnp.asarray(HEAD_DIM ** -0.5, q_pair.dtype)
            none = jnp.zeros_like(q_pair)
            key_at, value_at = ((0, 256), (128, 384), (512, 512))[pair]
            q_both = jnp.where(low, q_pair, none)
            if pair < 2:
                q_both = jnp.concatenate([q_both, jnp.where(low, none, q_pair)], axis=0)
            scores = dot_t(q_both, buf[window, key_at:key_at + 128]) + bias
            top = jnp.max(scores, axis=-1, keepdims=True)
            weights = jnp.exp(scores - top)
            total = jnp.sum(weights, axis=-1, keepdims=True)
            summed = dot(weights.astype(jnp.bfloat16), buf[window, value_at:value_at + 128]) / total
            if pair < 2:
                merged = jnp.where(low, summed[:BLK], summed[BLK:])
                out_ref[i * BLK:(i + 1) * BLK, pair * 128:(pair + 1) * 128] = merged.astype(jnp.bfloat16)
            else:
                out_ref[i * BLK:(i + 1) * BLK, 256:] = summed[:, HEAD_DIM:].astype(jnp.bfloat16)


def query_kernel(normed_ref, w_ref, kv_in, w_down_in, q_ref, kv_ref, w_down_ref):
    q_ref[...] = jnp.zeros_like(q_ref)
    q_ref[:, :w_ref.shape[1]] = dot_t(normed_ref[...], w_ref[0]).astype(jnp.bfloat16)
    kv_ref[...] = kv_in[...]
    w_down_ref[...] = w_down_in[...]


def last_row(ref):
    rows, width = ref.shape
    row = ref[rows - 8:, :][7:8]
    pieces = [row[:, g * 128:(g + 1) * 128] for g in range(width // 128)]
    pieces.append(jnp.zeros((IDROWS - len(pieces), 128), row.dtype))
    return jnp.concatenate(pieces, axis=0)


def mlp_kernel(tp_ref, core_ref, att0, att1, att2, att3, w_out_ref, *refs):
    pieces, frames_ref, gain_ref, w_up_ref, w_down_ref = refs[:6], *refs[6:10]
    resid_ref, part0, part1, part2, part3 = refs[10:15]
    resid_all, part_all = refs[15:]
    tp = tp_ref[0]
    rows = att0.shape[0]
    share = rows // 4
    half = pieces[0].shape[1]
    resid_all[...] = frames_ref[...].astype(jnp.float32) + dot(att0[...], w_out_ref[...])
    for n, side in enumerate((core_ref[0], 1 - core_ref[0])):
        columns = pl.ds(pl.multiple_of(side * half, half), half)
        term = resid_all[:, columns]
        for k, att in enumerate((att1, att2, att3)):
            term = term + dot(att[...], pieces[3 * n + k][...])
        resid_all[:, columns] = term
    resid = resid_all[...]
    normed = layer_norm(resid, gain_ref[...][None]).astype(jnp.bfloat16)
    hidden = gelu(dot(normed, w_up_ref[...])).astype(jnp.bfloat16)
    part_all[...] = dot(hidden, w_down_ref[...])
    mine = pl.ds(pl.multiple_of(tp * share, share), share)
    groups = resid_all.shape[1] // 128
    resid_ref[groups * share:, :] = last_row(resid_all)
    last = last_row(part_all).astype(jnp.bfloat16)
    for g in range(groups):
        resid_ref[g * share:(g + 1) * share, :] = resid_all[mine, g * 128:(g + 1) * 128]
    for k, part in enumerate((part0, part1, part2, part3)):
        target = pl.ds(pl.multiple_of(lax.rem(tp + k, 4) * share, share), share)
        for g in range(groups):
            part[g * share:(g + 1) * share, :] = part_all[target, g * 128:(g + 1) * 128].astype(jnp.bfloat16)
        part[groups * share:, :] = last


def layer_sum_kernel(resid_ref, own, got1, got2, got3, out_ref, rim_ref):
    total = resid_ref[...] + own[...].astype(jnp.float32)
    for piece in (got1, got2, got3):
        total = total + piece[...].astype(jnp.float32)
    share, width = out_ref.shape
    groups = width // 128
    for g in range(groups):
        out_ref[:, g * 128:(g + 1) * 128] = total[g * share:(g + 1) * share].astype(jnp.bfloat16)
    rim_ref[...] = total[groups * share:].astype(jnp.bfloat16)


def adapter_kernel(tp_ref, ids_ref, joined_ref, own, got1, got2, got3, rim_ref, w_conv_ref, w_proj_ref,
                   lm0, lm1, lm2, lm3, rows_ref, pooled_ref):
    tp = tp_ref[0]
    share = own.shape[0]
    for k, piece in enumerate((own, got1, got2, got3)):
        source = lax.rem(tp + 4 - k, 4)
        rows_ref[pl.ds(pl.multiple_of(source * share, share), share), :] = piece[...]
    rows = rows_ref[...]
    count = rows.shape[0] // 2
    j = lax.broadcasted_iota(jnp.int32, (count, 2 * count), 0)
    r = lax.broadcasted_iota(jnp.int32, (count, 2 * count), 1)
    same_block = ids_ref[0] == ids_ref[1]
    cut = jnp.where(same_block, -1, count // 2)
    one = lambda flag: jnp.where(flag, 1.0, 0.0).astype(jnp.bfloat16)
    picks = [one(r == 2 * j), one(r == 2 * j + 1), one((r == 2 * j - 1) & (j != cut))]
    picked = dot(jnp.concatenate(picks, axis=0), rows)
    even = picked[:count].astype(jnp.bfloat16)
    odd = picked[count:2 * count].astype(jnp.bfloat16)
    before = picked[2 * count:]
    rim = rim_ref[...].astype(jnp.float32)
    rim = jnp.concatenate([rim[g:g + 1] for g in range(before.shape[1] // 128)], axis=1)
    rim_first = jnp.where(joined_ref[0] == 1, 0, -1)
    top_row = lax.broadcasted_iota(jnp.int32, before.shape, 0) == rim_first
    before = before + jnp.where(top_row, rim, 0.0)
    conv = dot_t(before.astype(jnp.bfloat16), w_conv_ref[0])
    conv = conv + dot_t(even, w_conv_ref[1])
    conv = conv + dot_t(odd, w_conv_ref[2])
    pooled_ref[...] = gelu(conv).astype(jnp.bfloat16)
    piece = count // 4
    turned = [pooled_ref[pl.ds(pl.multiple_of(lax.rem(tp + k, 4) * piece, piece), piece), :] for k in range(4)]
    lm = dot(jnp.concatenate(turned, axis=0), w_proj_ref[...]).astype(jnp.bfloat16)
    for k, out in enumerate((lm0, lm1, lm2, lm3)):
        out[...] = lm[k * piece:(k + 1) * piece]


def lm_sum_kernel(own, got1, got2, got3, out_ref):
    total = own[...].astype(jnp.float32)
    for piece in (got1, got2, got3):
        total = total + piece[...].astype(jnp.float32)
    out_ref[...] = total.astype(jnp.bfloat16)


def params(mib):
    return pltpu.CompilerParams(vmem_limit_bytes=mib << 20)


def cost(flops, moved):
    return pl.CostEstimate(flops=int(flops), bytes_accessed=int(moved), transcendentals=0)


def bf16(*shape):
    return jax.ShapeDtypeStruct(shape, jnp.bfloat16)


def attend(ids, core, normed, w_qkv, kv, w_mine, w_down):
    rows = normed.shape[0]
    width = w_qkv.shape[1]
    back, on = send_chip(kv, 1), send_chip(kv, -1)
    w_two = send_tp(w_mine, 2)
    whole = lambda array: pl.BlockSpec(array.shape, lambda i: (0,) * array.ndim)
    queries, kv_held, w_down = pl.pallas_call(
        query_kernel,
        grid=(1,),
        out_shape=[bf16(rows, 384), bf16(*kv.shape), bf16(*w_down.shape)],
        in_specs=[whole(normed), pl.BlockSpec((1,) + w_qkv.shape[1:], lambda i: (0, 0, 0)), VMEM, VMEM],
        out_specs=[pl.BlockSpec((rows, 384), lambda i: (0, 0)), VMEM, VMEM],
        compiler_params=params(4),
        cost_estimate=cost(2e8, 2e6),
    )(normed, w_qkv, kv, w_down)
    back, kv_late = lax.optimization_barrier((back, kv))
    five = send_five(kv_late)
    far_back, far_on = send_chip(back, 1), send_chip(on, -1)
    w_one, w_three = send_pair(w_mine, 1), send_pair(w_mine, -1)
    far_back, far_on, w_two, w_one, five = lax.optimization_barrier((far_back, far_on, w_two, w_one, five))
    back_again, on_again, kv_again, queries = lax.optimization_barrier((back, on, kv_held, queries))
    beside = send_partner(kv_again)
    chain = [far_back, back, kv_held, on, far_on]
    swapped = [send_partner(far_back), send_partner(back_again), beside, send_partner(on_again), send_partner(far_on)]
    return pl.pallas_call(
        attend_kernel,
        out_shape=(bf16(rows, width), jax.ShapeDtypeStruct((1,), jnp.int32)),
        in_specs=[SMEM, SMEM, VMEM] + [ANY] * 11,
        out_specs=(VMEM, SMEM),
        scratch_shapes=[
            pltpu.VMEM((12 * rows, kv.shape[1]), jnp.bfloat16),
            pltpu.VMEM((12, IDROWS, 128), jnp.bfloat16),
            pltpu.SemaphoreType.DMA((11,)),
            pltpu.SemaphoreType.DMA((11,)),
        ],
        compiler_params=params(14),
        cost_estimate=cost(1e9, 4e6),
    )(ids, core, queries, *chain, *swapped, five), [w_one, w_two, w_three], w_down


def exchange(parts):
    far = send_tp(parts[1], 2)
    return [send_tp(parts[0], 1), far, send_tp(parts[2], 3)]


def shards(frames, gain_attn, w_qkv, w_out, gain_ffn, w_up, w_down, w_conv, w_proj, block_utt):
    rows, width = frames.shape
    share = rows // 4
    lm_width = w_proj.shape[1]
    w_qkv = jnp.swapaxes(w_qkv, 1, 2)
    w_conv = jnp.swapaxes(w_conv, 1, 2)
    tp = lax.axis_index(TP).astype(jnp.int32)[None]
    core = lax.rem(lax.axis_index(SEQ), 2).astype(jnp.int32)[None]
    scalar = jax.ShapeDtypeStruct((1,), jnp.int32)
    core, tp, normed, kv, w_mine = pl.pallas_call(
        kv_kernel,
        out_shape=(scalar, scalar, bf16(rows, width), bf16(rows + IDROWS, 2 * w_qkv.shape[1]), bf16(w_out.shape[0], width // 2)),
        in_specs=[SMEM, SMEM, SMEM, HBM, VMEM, HBM, HBM],
        out_specs=(SMEM, SMEM, ANY, VMEM, VMEM),
        scratch_shapes=[
            pltpu.VMEM((rows, width), jnp.bfloat16),
            pltpu.VMEM((2,) + w_qkv.shape[1:], jnp.bfloat16),
            pltpu.VMEM((rows, width), jnp.bfloat16),
            pltpu.SemaphoreType.DMA((5,)),
        ],
        compiler_params=params(56),
        cost_estimate=cost(4e8, 4e6),
    )(block_utt, core, tp, frames, gain_attn, w_qkv, w_out)
    (attended, joined), w_mine, w_down = attend(block_utt, core, normed, w_qkv, kv, w_mine, w_down)
    w_other = [send_partner(piece) for piece in reversed(w_mine)]
    attended, *w_other = lax.optimization_barrier((attended, *w_other))
    heads = [send_pair(attended, 1), send_tp(attended, 2), send_pair(attended, -1)]

    tall = share * (width // 128) + IDROWS
    resid, *parts = pl.pallas_call(
        mlp_kernel,
        out_shape=[jax.ShapeDtypeStruct((tall, 128), jnp.float32)] + [bf16(tall, 128)] * 4,
        in_specs=[SMEM] * 2 + [VMEM] * 15,
        out_specs=[VMEM] * 5,
        scratch_shapes=[pltpu.VMEM((rows, width), jnp.float32)] * 2,
        compiler_params=params(14),
        cost_estimate=cost(2.5e9, 1e7),
    )(tp, core, attended, *heads, w_out, *w_mine, *w_other, frames, gain_ffn, w_up, w_down)
    own, rim = pl.pallas_call(
        layer_sum_kernel,
        out_shape=[bf16(share, width), bf16(IDROWS, 128)],
        in_specs=[VMEM] * 5,
        out_specs=[VMEM] * 2,
        compiler_params=params(4),
        cost_estimate=cost(1e6, 1e6),
    )(resid, parts[0], *exchange(parts[1:]))
    layer = exchange([own] * 3)
    rim = send_seq(rim, 1)
    pooled_count = rows // 2
    lm = pl.pallas_call(
        adapter_kernel,
        out_shape=[bf16(pooled_count // 4, lm_width)] * 4,
        in_specs=[SMEM] * 3 + [VMEM] * 7,
        out_specs=[VMEM] * 4,
        scratch_shapes=[pltpu.VMEM((rows, width), jnp.bfloat16), pltpu.VMEM((pooled_count, w_conv.shape[1]), jnp.bfloat16)],
        compiler_params=params(10),
        cost_estimate=cost(1e9, 6e6),
    )(tp, block_utt, joined, own, *layer, rim, w_conv, w_proj)
    return pl.pallas_call(
        lm_sum_kernel,
        out_shape=bf16(pooled_count // 4, lm_width),
        in_specs=[VMEM] * 4,
        out_specs=VMEM,
        compiler_params=params(4),
        cost_estimate=cost(1e6, 1e6),
    )(lm[0], *exchange(lm[1:]))


def solution(mesh):
    placed = (
        P("seq", None),
        P(),
        P(None, None, "tp"),
        P("tp", None),
        P(),
        P(None, "tp"),
        P("tp", None),
        P(None, None, "tp"),
        P("tp", None),
        P("seq"),
    )
    return jax.shard_map(
        shards, mesh=mesh, in_specs=placed, out_specs=P(("seq", "tp"), None), check_vma=False
    )
```

```python
import jax
import jax.numpy as jnp
from jax import lax
from jax.experimental import pallas as pl
from jax.experimental.pallas import tpu as pltpu
from jax.sharding import PartitionSpec as P

HEAD_DIM = 64
BLK = 128
MOST = 11
IDROWS = 16
SEQ = "seq"
TP = "tp"
VMEM = pl.BlockSpec(memory_space=pltpu.VMEM)
SMEM = pl.BlockSpec(memory_space=pltpu.SMEM)
ANY = pl.BlockSpec(memory_space=pl.ANY)
HBM = pl.BlockSpec(memory_space=pltpu.HBM)


def send_tp(value, steps):
    count = lax.axis_size(TP)
    return lax.ppermute(value, TP, [(t, (t + steps) % count) for t in range(count)])


def send_pair(value, turn):
    seq, count = lax.axis_size(SEQ), lax.axis_size(TP)
    pairs = [(s * count + t, s * count + (t + turn * (-1 if s % 2 else 1)) % count) for s in range(seq) for t in range(count)]
    return lax.ppermute(value, (SEQ, TP), pairs)


def send_seq(value, steps):
    count = lax.axis_size(SEQ)
    return lax.ppermute(
        value, SEQ, [(s, s + steps) for s in range(count) if 0 <= s + steps < count]
    )


def send_chip(value, turn):
    count = lax.axis_size(SEQ)
    pairs = [(s, s + 2 * turn * (1 if s % 2 else -1)) for s in range(count)]
    return lax.ppermute(value, SEQ, [(a, b) for a, b in pairs if 0 <= b < count])


def send_partner(value):
    count = lax.axis_size(SEQ)
    return lax.ppermute(value, SEQ, [(s, s ^ 1) for s in range(count)])


def send_five(value):
    count = lax.axis_size(SEQ)
    pairs = [(s, s + 5 if s % 2 else s - 5) for s in range(count)]
    return lax.ppermute(value, SEQ, [(a, b) for a, b in pairs if 0 <= b < count])


def layer_norm(value, gain):
    mean = jnp.mean(value, axis=-1, keepdims=True)
    centred = value - mean
    spread = jnp.mean(centred * centred, axis=-1, keepdims=True)
    return centred * lax.rsqrt(spread + 1e-05) * gain


def dot_t(left, right):
    return lax.dot_general(left, right, (((1,), (1,)), ((), ())), preferred_element_type=jnp.float32)


def dot(left, right):
    return jnp.dot(left, right, preferred_element_type=jnp.float32)


def gelu(value):
    return 0.5 * value * (1.0 + lax.erf(value * (0.5 ** 0.5)))


def kv_kernel(ids_ref, core_ref, tp_ref, frames_hbm, gain_ref, w_hbm, w_out_hbm,
              core_out, tp_out, normed_out, kv_ref, w_mine_ref,
              frames_ref, w_ref, normed_ref, sems):
    rows = frames_ref.shape[0]
    core_out[0] = core_ref[0]
    tp_out[0] = tp_ref[0]
    copies = [pltpu.make_async_copy(frames_hbm, frames_ref, sems.at[0])]
    copies += [pltpu.make_async_copy(w_hbm.at[k], w_ref.at[k - 1], sems.at[k]) for k in (1, 2)]
    half = w_mine_ref.shape[1]
    copies.append(pltpu.make_async_copy(
        w_out_hbm.at[:, pl.ds(pl.multiple_of(core_ref[0] * half, half), half)], w_mine_ref, sems.at[3]))
    for copy in copies:
        copy.start()
    copies[0].wait()
    normed = layer_norm(frames_ref[...].astype(jnp.float32), gain_ref[...][None]).astype(jnp.bfloat16)
    normed_ref[...] = normed
    copies.append(pltpu.make_async_copy(normed_ref, normed_out, sems.at[4]))
    copies[4].start()
    copies[1].wait()
    keys = dot_t(normed, w_ref[0]).astype(jnp.bfloat16)
    copies[2].wait()
    values = dot_t(normed, w_ref[1]).astype(jnp.bfloat16)
    kv_ref[:rows, :256] = keys[:, :256]
    kv_ref[:rows, 256:512] = values[:, :256]
    kv_ref[:rows, 512:576] = keys[:, 256:]
    kv_ref[:rows, 576:] = values[:, 256:]
    row = lax.broadcasted_iota(jnp.int32, (IDROWS, kv_ref.shape[1]), 0)
    marks = jnp.where(row == 0, ids_ref[0] + 1, jnp.where(row == 1, ids_ref[1] + 1, 0))
    kv_ref[rows:, :] = marks.astype(jnp.float32).astype(jnp.bfloat16)
    copies[3].wait()
    copies[4].wait()


def attend_kernel(ids_ref, core_ref, q_ref, *refs):
    pieces, (out_ref, joined_ref, buf, marks, sems, mark_sems) = refs[:11], refs[11:]
    parity = core_ref[0]
    rows = q_ref.shape[0]
    copies = []
    for n, piece in enumerate(pieces):
        slot = (9 - 7 * parity, 7 - 3 * parity, 5 + parity, 3 + 5 * parity, 1 + 9 * parity,
                2 + 7 * parity, 4 + 3 * parity, 6 - parity, 8 - 5 * parity, 10 - 9 * parity, 11 * parity)[n]
        copies.append(pltpu.make_async_copy(
            piece.at[pl.ds(rows, IDROWS), pl.ds(0, 128)], marks.at[slot], mark_sems.at[n]))
        copies.append(pltpu.make_async_copy(
            piece.at[pl.ds(0, rows), :], buf.at[pl.ds(pl.multiple_of(slot * rows, rows), rows), :], sems.at[n]))
    for copy in copies:
        copy.start()
    unused = 11 - 11 * parity
    marks[unused] = jnp.zeros(marks.shape[1:], marks.dtype)
    for copy in copies:
        copy.wait()
    seen = marks[...].astype(jnp.float32)
    row = lax.broadcasted_iota(jnp.int32, seen.shape, 1)
    place = (2 * lax.broadcasted_iota(jnp.int32, seen.shape, 0) + row).astype(jnp.float32)
    lane = lax.broadcasted_iota(jnp.int32, (BLK, 128), 1)
    column = lax.broadcasted_iota(jnp.int32, (1, MOST * BLK), 1)
    low = lane < HEAD_DIM
    for i in range(2):
        mine = (ids_ref[i] + 1).astype(jnp.float32)
        same = (seen == mine) & (row < 2)
        first = jnp.min(jnp.where(same, place, 99.0)).astype(jnp.int32)
        last = jnp.max(jnp.where(same, place, -1.0)).astype(jnp.int32)
        if i == 0:
            joined_ref[0] = (first < 10 + 2 * parity).astype(jnp.int32)
        start = jnp.clip(first, 2 * parity, MOST + 2 * parity)
        begin = pl.multiple_of(start * BLK, BLK)
        kept = (last + 1 - start) * BLK
        bias = jnp.where(column < kept, 0.0, -1e30)
        window = pl.ds(begin, MOST * BLK)
        for pair in range(3):
            q_pair = q_ref[i * BLK:(i + 1) * BLK, pair * 128:(pair + 1) * 128]
            none = jnp.zeros_like(q_pair)
            key_at, value_at = ((0, 256), (128, 384), (512, 512))[pair]
            q_both = jnp.where(low, q_pair, none)
            if pair < 2:
                q_both = jnp.concatenate([q_both, jnp.where(low, none, q_pair)], axis=0)
            scores = dot_t(q_both, buf[window, key_at:key_at + 128]) + bias
            top = jnp.max(scores, axis=-1, keepdims=True)
            weights = jnp.exp(scores - top)
            total = jnp.sum(weights, axis=-1, keepdims=True)
            summed = dot(weights.astype(jnp.bfloat16), buf[window, value_at:value_at + 128]) / total
            if pair < 2:
                merged = jnp.where(low, summed[:BLK], summed[BLK:])
                out_ref[i * BLK:(i + 1) * BLK, pair * 128:(pair + 1) * 128] = merged.astype(jnp.bfloat16)
            else:
                out_ref[i * BLK:(i + 1) * BLK, 256:] = summed[:, HEAD_DIM:].astype(jnp.bfloat16)


def query_kernel(normed_ref, w_ref, kv_in, w_down_in, q_ref, kv_ref, w_down_ref):
    q_ref[...] = jnp.zeros_like(q_ref)
    queries = dot_t(normed_ref[...], w_ref[0]).astype(jnp.bfloat16)
    q_ref[:, :w_ref.shape[1]] = queries * jnp.asarray(HEAD_DIM ** -0.5, jnp.bfloat16)
    kv_ref[...] = kv_in[...]
    w_down_ref[...] = w_down_in[...]


def last_row(ref):
    rows, width = ref.shape
    row = ref[rows - 8:, :][7:8]
    pieces = [row[:, g * 128:(g + 1) * 128] for g in range(width // 128)]
    pieces.append(jnp.zeros((IDROWS - len(pieces), 128), row.dtype))
    return jnp.concatenate(pieces, axis=0)


def mlp_kernel(tp_ref, core_ref, att0, att1, att2, att3, w_out_ref, *refs):
    pieces, frames_ref, gain_ref, w_up_ref, w_down_ref = refs[:6], *refs[6:10]
    resid_ref, part0, part1, part2, part3 = refs[10:15]
    resid_all, part_all = refs[15:]
    tp = tp_ref[0]
    rows = att0.shape[0]
    share = rows // 4
    half = pieces[0].shape[1]
    resid_all[...] = frames_ref[...].astype(jnp.float32) + dot(att0[...], w_out_ref[...])
    for n, side in enumerate((core_ref[0], 1 - core_ref[0])):
        columns = pl.ds(pl.multiple_of(side * half, half), half)
        term = resid_all[:, columns]
        for k, att in enumerate((att1, att2, att3)):
            term = term + dot(att[...], pieces[3 * n + k][...])
        resid_all[:, columns] = term
    resid = resid_all[...]
    normed = layer_norm(resid, gain_ref[...][None]).astype(jnp.bfloat16)
    hidden = gelu(dot(normed, w_up_ref[...])).astype(jnp.bfloat16)
    part_all[...] = dot(hidden, w_down_ref[...])
    mine = pl.ds(pl.multiple_of(tp * share, share), share)
    groups = resid_all.shape[1] // 128
    resid_ref[groups * share:, :] = last_row(resid_all)
    last = last_row(part_all).astype(jnp.bfloat16)
    for g in range(groups):
        resid_ref[g * share:(g + 1) * share, :] = resid_all[mine, g * 128:(g + 1) * 128]
    for k, part in enumerate((part0, part1, part2, part3)):
        target = pl.ds(pl.multiple_of(lax.rem(tp + k, 4) * share, share), share)
        for g in range(groups):
            part[g * share:(g + 1) * share, :] = part_all[target, g * 128:(g + 1) * 128].astype(jnp.bfloat16)
        part[groups * share:, :] = last


def layer_sum_kernel(resid_ref, own, got1, got2, got3, out_ref, rim_ref):
    total = resid_ref[...] + own[...].astype(jnp.float32)
    for piece in (got1, got2, got3):
        total = total + piece[...].astype(jnp.float32)
    share, width = out_ref.shape
    groups = width // 128
    for g in range(groups):
        out_ref[:, g * 128:(g + 1) * 128] = total[g * share:(g + 1) * share].astype(jnp.bfloat16)
    rim_ref[...] = total[groups * share:].astype(jnp.bfloat16)


def adapter_kernel(tp_ref, ids_ref, joined_ref, own, got1, got2, got3, rim_ref, w_conv_ref, w_proj_ref,
                   lm0, lm1, lm2, lm3, rows_ref, pooled_ref):
    tp = tp_ref[0]
    share = own.shape[0]
    for k, piece in enumerate((own, got1, got2, got3)):
        source = lax.rem(tp + 4 - k, 4)
        rows_ref[pl.ds(pl.multiple_of(source * share, share), share), :] = piece[...]
    rows = rows_ref[...]
    count = rows.shape[0] // 2
    j = lax.broadcasted_iota(jnp.int32, (count, 2 * count), 0)
    r = lax.broadcasted_iota(jnp.int32, (count, 2 * count), 1)
    same_block = ids_ref[0] == ids_ref[1]
    cut = jnp.where(same_block, -1, count // 2)
    one = lambda flag: jnp.where(flag, 1.0, 0.0).astype(jnp.bfloat16)
    picks = [one(r == 2 * j), one(r == 2 * j + 1), one((r == 2 * j - 1) & (j != cut))]
    picked = dot(jnp.concatenate(picks, axis=0), rows)
    even = picked[:count].astype(jnp.bfloat16)
    odd = picked[count:2 * count].astype(jnp.bfloat16)
    before = picked[2 * count:]
    rim = rim_ref[...].astype(jnp.float32)
    rim = jnp.concatenate([rim[g:g + 1] for g in range(before.shape[1] // 128)], axis=1)
    rim_first = jnp.where(joined_ref[0] == 1, 0, -1)
    top_row = lax.broadcasted_iota(jnp.int32, before.shape, 0) == rim_first
    before = before + jnp.where(top_row, rim, 0.0)
    conv = dot_t(before.astype(jnp.bfloat16), w_conv_ref[0])
    conv = conv + dot_t(even, w_conv_ref[1])
    conv = conv + dot_t(odd, w_conv_ref[2])
    pooled_ref[...] = gelu(conv).astype(jnp.bfloat16)
    piece = count // 4
    turned = [pooled_ref[pl.ds(pl.multiple_of(lax.rem(tp + k, 4) * piece, piece), piece), :] for k in range(4)]
    lm = dot(jnp.concatenate(turned, axis=0), w_proj_ref[...]).astype(jnp.bfloat16)
    for k, out in enumerate((lm0, lm1, lm2, lm3)):
        out[...] = lm[k * piece:(k + 1) * piece]


def lm_sum_kernel(own, got1, got2, got3, out_ref):
    total = own[...].astype(jnp.float32)
    for piece in (got1, got2, got3):
        total = total + piece[...].astype(jnp.float32)
    out_ref[...] = total.astype(jnp.bfloat16)


def params(mib):
    return pltpu.CompilerParams(vmem_limit_bytes=mib << 20)


def cost(flops, moved):
    return pl.CostEstimate(flops=int(flops), bytes_accessed=int(moved), transcendentals=0)


def bf16(*shape):
    return jax.ShapeDtypeStruct(shape, jnp.bfloat16)


def attend(ids, core, normed, w_qkv, kv, w_mine, w_down):
    rows = normed.shape[0]
    width = w_qkv.shape[1]
    back, on = send_chip(kv, 1), send_chip(kv, -1)
    w_two = send_tp(w_mine, 2)
    whole = lambda array: pl.BlockSpec(array.shape, lambda i: (0,) * array.ndim)
    queries, kv_held, w_down = pl.pallas_call(
        query_kernel,
        grid=(1,),
        out_shape=[bf16(rows, 384), bf16(*kv.shape), bf16(*w_down.shape)],
        in_specs=[whole(normed), pl.BlockSpec((1,) + w_qkv.shape[1:], lambda i: (0, 0, 0)), VMEM, VMEM],
        out_specs=[pl.BlockSpec((rows, 384), lambda i: (0, 0)), VMEM, VMEM],
        compiler_params=params(4),
        cost_estimate=cost(2e8, 2e6),
    )(normed, w_qkv, kv, w_down)
    back, kv_late = lax.optimization_barrier((back, kv))
    five = send_five(kv_late)
    far_back, far_on = send_chip(back, 1), send_chip(on, -1)
    w_one, w_three = send_pair(w_mine, 1), send_pair(w_mine, -1)
    far_back, far_on, w_two, w_one, five = lax.optimization_barrier((far_back, far_on, w_two, w_one, five))
    back_again, on_again, kv_again, queries = lax.optimization_barrier((back, on, kv_held, queries))
    beside = send_partner(kv_again)
    chain = [far_back, back, kv_held, on, far_on]
    swapped = [send_partner(far_back), send_partner(back_again), beside, send_partner(on_again), send_partner(far_on)]
    return pl.pallas_call(
        attend_kernel,
        out_shape=(bf16(rows, width), jax.ShapeDtypeStruct((1,), jnp.int32)),
        in_specs=[SMEM, SMEM, VMEM] + [ANY] * 11,
        out_specs=(VMEM, SMEM),
        scratch_shapes=[
            pltpu.VMEM((12 * rows, kv.shape[1]), jnp.bfloat16),
            pltpu.VMEM((12, IDROWS, 128), jnp.bfloat16),
            pltpu.SemaphoreType.DMA((11,)),
            pltpu.SemaphoreType.DMA((11,)),
        ],
        compiler_params=params(14),
        cost_estimate=cost(1e9, 4e6),
    )(ids, core, queries, *chain, *swapped, five), [w_one, w_two, w_three], w_down


def exchange(parts):
    far = send_tp(parts[1], 2)
    return [send_tp(parts[0], 1), far, send_tp(parts[2], 3)]


def shards(frames, gain_attn, w_qkv, w_out, gain_ffn, w_up, w_down, w_conv, w_proj, block_utt):
    rows, width = frames.shape
    share = rows // 4
    lm_width = w_proj.shape[1]
    w_qkv = jnp.swapaxes(w_qkv, 1, 2)
    w_conv = jnp.swapaxes(w_conv, 1, 2)
    tp = lax.axis_index(TP).astype(jnp.int32)[None]
    core = lax.rem(lax.axis_index(SEQ), 2).astype(jnp.int32)[None]
    scalar = jax.ShapeDtypeStruct((1,), jnp.int32)
    core, tp, normed, kv, w_mine = pl.pallas_call(
        kv_kernel,
        out_shape=(scalar, scalar, bf16(rows, width), bf16(rows + IDROWS, 2 * w_qkv.shape[1]), bf16(w_out.shape[0], width // 2)),
        in_specs=[SMEM, SMEM, SMEM, HBM, VMEM, HBM, HBM],
        out_specs=(SMEM, SMEM, ANY, VMEM, VMEM),
        scratch_shapes=[
            pltpu.VMEM((rows, width), jnp.bfloat16),
            pltpu.VMEM((2,) + w_qkv.shape[1:], jnp.bfloat16),
            pltpu.VMEM((rows, width), jnp.bfloat16),
            pltpu.SemaphoreType.DMA((5,)),
        ],
        compiler_params=params(56),
        cost_estimate=cost(4e8, 4e6),
    )(block_utt, core, tp, frames, gain_attn, w_qkv, w_out)
    (attended, joined), w_mine, w_down = attend(block_utt, core, normed, w_qkv, kv, w_mine, w_down)
    w_other = [send_partner(piece) for piece in reversed(w_mine)]
    attended, *w_other = lax.optimization_barrier((attended, *w_other))
    heads = [send_pair(attended, 1), send_tp(attended, 2), send_pair(attended, -1)]

    tall = share * (width // 128) + IDROWS
    resid, *parts = pl.pallas_call(
        mlp_kernel,
        out_shape=[jax.ShapeDtypeStruct((tall, 128), jnp.float32)] + [bf16(tall, 128)] * 4,
        in_specs=[SMEM] * 2 + [VMEM] * 15,
        out_specs=[VMEM] * 5,
        scratch_shapes=[pltpu.VMEM((rows, width), jnp.float32)] * 2,
        compiler_params=params(14),
        cost_estimate=cost(2.5e9, 1e7),
    )(tp, core, attended, *heads, w_out, *w_mine, *w_other, frames, gain_ffn, w_up, w_down)
    own, rim = pl.pallas_call(
        layer_sum_kernel,
        out_shape=[bf16(share, width), bf16(IDROWS, 128)],
        in_specs=[VMEM] * 5,
        out_specs=[VMEM] * 2,
        compiler_params=params(4),
        cost_estimate=cost(1e6, 1e6),
    )(resid, parts[0], *exchange(parts[1:]))
    layer = exchange([own] * 3)
    rim = send_seq(rim, 1)
    pooled_count = rows // 2
    lm = pl.pallas_call(
        adapter_kernel,
        out_shape=[bf16(pooled_count // 4, lm_width)] * 4,
        in_specs=[SMEM] * 3 + [VMEM] * 7,
        out_specs=[VMEM] * 4,
        scratch_shapes=[pltpu.VMEM((rows, width), jnp.bfloat16), pltpu.VMEM((pooled_count, w_conv.shape[1]), jnp.bfloat16)],
        compiler_params=params(10),
        cost_estimate=cost(1e9, 6e6),
    )(tp, block_utt, joined, own, *layer, rim, w_conv, w_proj)
    return pl.pallas_call(
        lm_sum_kernel,
        out_shape=bf16(pooled_count // 4, lm_width),
        in_specs=[VMEM] * 4,
        out_specs=VMEM,
        compiler_params=params(4),
        cost_estimate=cost(1e6, 1e6),
    )(lm[0], *exchange(lm[1:]))


def solution(mesh):
    placed = (
        P("seq", None),
        P(),
        P(None, None, "tp"),
        P("tp", None),
        P(),
        P(None, "tp"),
        P("tp", None),
        P(None, None, "tp"),
        P("tp", None),
        P("seq"),
    )
    return jax.shard_map(
        shards, mesh=mesh, in_specs=placed, out_specs=P(("seq", "tp"), None), check_vma=False
    )
```
